128 devices in a mesh: row: 16 (over z, y), col: 8 (over x, core).
Axes of the slice: x: 4, y: 4, z: 4, core: 2. Of those that a mesh axis runs over, the one named last changes fastest.
Arguments:
- tokens: bfloat16 [1024, 8192], P('row', 'col'), may hold values from -6 to 6
- cotangent: bfloat16 [1024, 8192], P('row', 'col'), may hold values from -3 to 3
- gate_weight: bfloat16 [8192, 14336], P('col', 'row'), may hold values from -0.0625 to 0.0625
- up_weight: bfloat16 [8192, 14336], P('col', 'row'), may hold values from -0.0625 to 0.0625
- down_weight: bfloat16 [14336, 8192], P('row', 'col'), may hold values from -0.046875 to 0.046875
- gate_mask: int32 [64, 112], P('col', 'row'), may hold values from 0 to 1
- up_mask: int32 [64, 112], P('col', 'row'), may hold values from 0 to 1
- down_mask: int32 [112, 64], P('row', 'col'), may hold values from 0 to 1
Outputs:
- output: bfloat16 [1024, 8192], P('row', 'col')
- grad_tokens: bfloat16 [1024, 8192], P('row', 'col')
- grad_gate_weight: bfloat16 [8192, 14336], P('col', 'row')
- grad_up_weight: bfloat16 [8192, 14336], P('col', 'row')
- grad_down_weight: bfloat16 [14336, 8192], P('row', 'col')
The draws below stay inside these ranges and needn't reach their ends.
All inputs are finite; a program needn't handle non-finite values.
Results may differ from the reference program's by a relative error of at most 0.005.
Values may be sent and summed in bfloat16 or wider, within the bound.
A program may use at most 128 MiB of HBM per device.

```python
import jax
import jax.numpy as jnp

D = 8192
FF = 14336
BLOCK = 128
TOKENS = 1024


def block_pattern(key, row_count, col_count, along_columns):
    level_key, value_key = jax.random.split(key)
    if along_columns:
        levels = jax.random.randint(level_key, (1, col_count), 1, 8)
    else:
        levels = jax.random.randint(level_key, (row_count, 1), 1, 8)
    values = jax.random.randint(value_key, (row_count, col_count), 0, 8)
    return (values < levels).astype(jnp.int32)


def draw_gate_mask(key, part):
    key = jax.random.fold_in(key, 11)
    return block_pattern(key, D // BLOCK, FF // BLOCK, True)


def draw_up_mask(key, part):
    key = jax.random.fold_in(key, 23)
    return block_pattern(key, D // BLOCK, FF // BLOCK, True)


def draw_down_mask(key, part):
    key = jax.random.fold_in(key, 37)
    return block_pattern(key, FF // BLOCK, D // BLOCK, False)


def block_scale(key, dims, pieces, smallest, largest):
    def one(axis_at, parts):
        draws = jax.random.uniform(jax.random.fold_in(jax.random.fold_in(key, 6), axis_at), (parts,), jnp.float32, smallest / len(pieces), largest / len(pieces))
        return jnp.repeat(jnp.exp(draws), dims[axis_at] // parts).reshape((-1,) + (1,) * (len(dims) - axis_at - 1))

    level = one(*pieces[0])
    for cut in pieces[1:]:
        level = level * one(*cut)
    return level


def noise(stream_key, shape, spread, reach, shards=(), held_as=jnp.bfloat16):
    values = jax.random.normal(stream_key, shape, jnp.float32) * spread
    if len(shards) > 0:
        values = block_scale(stream_key, shape, shards, -0.22, 0.18) * values
    return jnp.clip(values, min=-reach, max=reach).astype(held_as)


def setup_inputs(seed: int = 0) -> dict:
    keys = jax.random.split(jax.random.key(seed), 9)
    return {
        "tokens": noise(keys[0], (TOKENS, D), 1.0, 6.0, ((0, 16), (1, 8))),
        "cotangent": noise(keys[1], (TOKENS, D), 0.5, 3.0, ((0, 16), (1, 8))),
        "gate_weight": noise(keys[2], (D, FF), D ** -0.5, 0.0625, ((0, 8), (1, 16))),
        "up_weight": noise(keys[3], (D, FF), D ** -0.5, 0.0625, ((0, 8), (1, 16))),
        "down_weight": noise(keys[4], (FF, D), FF ** -0.5, 0.046875, ((0, 16), (1, 8))),
        "gate_mask": draw_gate_mask(jax.random.fold_in(keys[8], 71), 0),
        "up_mask": draw_up_mask(jax.random.fold_in(keys[8], 71), 0),
        "down_mask": draw_down_mask(jax.random.fold_in(keys[8], 71), 0),
    }


def apply_blocks(weight, keep_mask):
    row_blocks, col_blocks = keep_mask.shape
    height = weight.shape[0] // row_blocks
    breadth = weight.shape[1] // col_blocks
    shaped = weight.reshape(row_blocks, height, col_blocks, breadth)
    return (shaped * keep_mask.astype(weight.dtype)[:, None, :, None]).reshape(weight.shape)


def reference(tokens, cotangent, gate_weight, up_weight, down_weight, gate_mask, up_mask, down_mask):
    gate_kept = apply_blocks(gate_weight, gate_mask)
    up_kept = apply_blocks(up_weight, up_mask)
    down_kept = apply_blocks(down_weight, down_mask)
    gate_values = jnp.dot(tokens, gate_kept, preferred_element_type=jnp.float32)
    up_values = jnp.dot(tokens, up_kept, preferred_element_type=jnp.float32)
    sigmoid_gate = jax.nn.sigmoid(gate_values)
    hidden = (gate_values * sigmoid_gate * up_values).astype(jnp.bfloat16)
    output = jnp.dot(hidden, down_kept, preferred_element_type=jnp.float32).astype(jnp.bfloat16)
    grad_hidden = jnp.dot(cotangent, down_kept.T, preferred_element_type=jnp.float32)
    grad_gate = (grad_hidden * up_values * sigmoid_gate * (1.0 + gate_values * (1.0 - sigmoid_gate))).astype(jnp.bfloat16)
    grad_up = (grad_hidden * gate_values * sigmoid_gate).astype(jnp.bfloat16)
    grad_tokens = (jnp.dot(grad_gate, gate_kept.T, preferred_element_type=jnp.float32)
                   + jnp.dot(grad_up, up_kept.T, preferred_element_type=jnp.float32)).astype(jnp.bfloat16)
    grad_gate_weight = apply_blocks(jnp.dot(tokens.T, grad_gate, preferred_element_type=jnp.float32), gate_mask).astype(jnp.bfloat16)
    grad_up_weight = apply_blocks(jnp.dot(tokens.T, grad_up, preferred_element_type=jnp.float32), up_mask).astype(jnp.bfloat16)
    grad_down_weight = apply_blocks(jnp.dot(hidden.T, cotangent, preferred_element_type=jnp.float32), down_mask).astype(jnp.bfloat16)
    return (output, grad_tokens, grad_gate_weight, grad_up_weight, grad_down_weight)
```

```python
import functools

import jax
import jax.numpy as jnp
from jax import lax
from jax.experimental import pallas as pl
from jax.experimental.pallas import tpu as pltpu
from jax.sharding import PartitionSpec as P

BLOCK = 128
MESH = pl.DeviceIdType.MESH
F32 = jnp.float32
BF16 = jnp.bfloat16


def column_tiles(width):
    return [(at, min(256, width - at)) for at in range(0, width, 256)]


def kernel(
    dims,
    tok_ref, cot_ref, gate_hbm, up_hbm, down_hbm, gate_mask, up_mask, down_mask,
    out_ref, grad_ref, dgate_hbm, dup_hbm, ddown_hbm,
    wg, wu, wd, act, part, rpart, xs, xr, hall, outp, r1, r2f, r2s, r2r, dg, du, dd,
    w_sem, dw_sem, ag1_s, ag1_r, ag2_s, ag2_r, cx_s, cx_r, rs_s, rs_r, gx_s, gx_r, cf_s, cf_r,
    p1_s, p1_r, p2_s, p2_r,
):
    Z, Y, X, N, R = dims
    T = Z * Y * R
    half = T // 2
    Q = half // X
    DL, FL = wg.shape
    row = lax.axis_index("row")
    col = lax.axis_index("col")
    z, y = row // Y, row % Y
    x, k = col // 2, col % 2

    def at_z(d):
        return (((z + d) % Z) * Y + y, col)

    def at_y(d):
        return (z * Y + (y + d) % Y, col)

    def at_x(d):
        return (row, ((x + d) % X) * 2 + k)

    other = (row, x * 2 + 1 - k)

    def remote(src, dst, ssem, rsem, where):
        return pltpu.make_async_remote_copy(
            src_ref=src, dst_ref=dst, send_sem=ssem, recv_sem=rsem, device_id=where, device_id_type=MESH
        )

    def ag1(c):
        mine = pl.ds(c * R, R)
        return [
            remote(tok_ref.at[mine], act.at[0, c, z, y], ag1_s.at[c, 0, d - 1], ag1_r.at[c, 0, d - 1], at_y(d))
            for d in range(1, Y)
        ] + [
            remote(cot_ref.at[mine], act.at[1, c, z, y], ag1_s.at[c, 1, d - 1], ag1_r.at[c, 1, d - 1], at_z(d))
            for d in range(1, Z)
        ]

    def ag2(c):
        tok = [
            remote(act.at[0, c, z], act.at[0, c, z], ag2_s.at[c, 0, d - 1], ag2_r.at[c, 0, d - 1], at_z(d))
            for d in range(1, Z)
        ]
        cot = [
            remote(act.at[1, c, :, y], act.at[1, c, :, y], ag2_s.at[c, 1, d - 1], ag2_r.at[c, 1, d - 1], at_y(d))
            for d in range(1, Y)
        ]
        return tok, cot

    def cx(c, j):
        return remote(
            part.at[c, j, pl.ds((1 - k) * half, half)], rpart.at[c, j], cx_s.at[c, j], cx_r.at[c, j], other
        )

    def rs(c):
        return [
            remote(xs.at[c, (x + d) % X], xr.at[c, d - 1], rs_s.at[c, d - 1], rs_r.at[c, d - 1], at_x(d))
            for d in range(1, X)
        ]

    def gx(c):
        mine = hall.at[c, k * X + x]
        return [remote(mine, mine, gx_s.at[c, d - 1], gx_r.at[c, d - 1], at_x(d)) for d in range(1, X)]

    def cf(c, d):
        block = hall.at[c, k * X + (x + X - d) % X]
        return remote(block, block, cf_s.at[c, d], cf_r.at[c, d], other)

    def p1(c):
        out = [
            remote(outp.at[c, 0, (z + d) % Z], r1.at[c, 0, d - 1], p1_s.at[c, 0, d - 1], p1_r.at[c, 0, d - 1], at_z(d))
            for d in range(1, Z)
        ]
        grad = [
            remote(outp.at[c, 1, :, (y + d) % Y], r1.at[c, 1, d - 1], p1_s.at[c, 1, d - 1], p1_r.at[c, 1, d - 1], at_y(d))
            for d in range(1, Y)
        ]
        return out, grad

    def p2(c):
        out = [
            remote(r2s.at[c, 0, (y + d) % Y], r2r.at[c, 0, d - 1], p2_s.at[c, 0, d - 1], p2_r.at[c, 0, d - 1], at_y(d))
            for d in range(1, Y)
        ]
        grad = [
            remote(r2s.at[c, 1, (z + d) % Z], r2r.at[c, 1, d - 1], p2_s.at[c, 1, d - 1], p2_r.at[c, 1, d - 1], at_z(d))
            for d in range(1, Z)
        ]
        return out, grad

    def start(copies):
        for copy in copies:
            copy.start()

    def recv(copies):
        for copy in copies:
            copy.wait_recv()

    loads = [
        pltpu.make_async_copy(src, dst, w_sem.at[i])
        for i, (src, dst) in enumerate(((gate_hbm, wg), (up_hbm, wu), (down_hbm, wd)))
    ]
    start(loads)
    peers = [other] + [at_x(d) for d in range(1, X)] + [at_y(d) for d in range(1, Y)] + [at_z(d) for d in range(1, Z)]
    barrier = pltpu.get_barrier_semaphore()
    for peer in peers:
        pl.semaphore_signal(barrier, inc=1, device_id=peer, device_id_type=MESH)
    pl.semaphore_wait(barrier, len(peers))

    start(ag1(0))
    for c in range(N):
        act[0, c, z, y] = tok_ref[c * R : (c + 1) * R, :]
        act[1, c, z, y] = cot_ref[c * R : (c + 1) * R, :]
    if N > 1:
        start(ag1(1))

    def gather_on(c):
        recv(ag1(c))
        tok, cot = ag2(c)
        start(tok)
        start(cot)

    gather_on(0)

    for copy, weight, mask in zip(loads, (wg, wu, wd), (gate_mask, up_mask, down_mask)):
        copy.wait()
        high, wide = weight.shape[0] // BLOCK, weight.shape[1] // BLOCK

        def keep_row(i, _, weight=weight, mask=mask, wide=wide):
            rows = pl.ds(pl.multiple_of(i * BLOCK, BLOCK), BLOCK)
            for j in range(wide):
                cols = slice(j * BLOCK, (j + 1) * BLOCK)
                kept = jnp.full((BLOCK, BLOCK), mask[i, j], jnp.int32).astype(F32).astype(BF16)
                weight[rows, cols] = weight[rows, cols] * kept
            return 0

        lax.fori_loop(0, high, keep_row, 0)

    def forward(c):
        tok, cot = ag2(c)
        recv(tok)
        for j, weight in enumerate((wg, wu)):
            tokens = act[0, c].reshape(T, DL)
            for at, width in column_tiles(FL):
                part[c, j, :, at : at + width] = jnp.dot(
                    tokens, weight[:, at : at + width], preferred_element_type=F32
                )
            cx(c, j).start()
        recv(cot)
        upstream = act[1, c].reshape(T, DL)
        for at, width in column_tiles(FL):
            part[c, 2, :, at : at + width] = lax.dot_general(
                upstream, wd[at : at + width, :], (((1,), (1,)), ((), ())), preferred_element_type=F32
            )
        cx(c, 2).start()

    def share(c):
        for j in range(3):
            cx(c, j).wait_recv()
            for b in range(X):
                total = part[c, j, pl.ds(k * half + b * Q, Q), :] + rpart[c, j, b * Q : (b + 1) * Q, :]
                xs[c, b, j] = total.astype(BF16)
        start(rs(c))

    def activate(c):
        recv(rs(c))

        def total(j):
            value = part[c, j, pl.ds(k * half + x * Q, Q), :] + rpart[c, j, pl.ds(x * Q, Q), :]
            for d in range(1, X):
                value = value + xr[c, d - 1, j].astype(F32)
            return value

        gate, up, back = total(0), total(1), total(2)
        s = 1.0 / (1.0 + jnp.exp(-gate))
        block = k * X + x
        hall[c, block, 0] = (gate * s * up).astype(BF16)
        hall[c, block, 1] = (back * up * s * (1.0 + gate * (1.0 - s))).astype(BF16)
        hall[c, block, 2] = (back * gate * s).astype(BF16)
        start(gx(c))
        cf(c, 0).start()

    def pass_on(c):
        for d, copy in enumerate(gx(c)):
            copy.wait_recv()
            cf(c, d + 1).start()

    def backward(c):
        for d in range(X):
            cf(c, d).wait_recv()
        out, grad = p1(c)
        hidden = hall[c, :, 0].reshape(T, FL)
        for at, width in column_tiles(DL):
            value = jnp.dot(hidden, wd[:, at : at + width], preferred_element_type=F32)
            outp[c, 0, :, :, :, at : at + width] = value.astype(BF16).reshape(Z, Y, R, width)
        start(out)
        grad_gate = hall[c, :, 1].reshape(T, FL)
        grad_up = hall[c, :, 2].reshape(T, FL)
        for at, width in column_tiles(DL):
            nt = (((1,), (1,)), ((), ()))
            value = lax.dot_general(grad_gate, wg[at : at + width, :], nt, preferred_element_type=F32)
            value += lax.dot_general(grad_up, wu[at : at + width, :], nt, preferred_element_type=F32)
            outp[c, 1, :, :, :, at : at + width] = value.astype(BF16).reshape(Z, Y, R, width)
        start(grad)

    def narrow(c):
        out, grad = p1(c)
        send_out, send_grad = p2(c)
        recv(out)
        for b in range(Y):
            value = outp[c, 0, z, b].astype(F32)
            for d in range(1, Z):
                value = value + r1[c, 0, d - 1, b].astype(F32)
            r2f[c, 0, b] = value
            r2s[c, 0, b] = value.astype(BF16)
        start(send_out)
        recv(grad)
        for b in range(Z):
            value = outp[c, 1, b, y].astype(F32)
            for d in range(1, Y):
                value = value + r1[c, 1, d - 1, b].astype(F32)
            r2f[c, 1, b] = value
            r2s[c, 1, b] = value.astype(BF16)
        start(send_grad)

    def finish(c):
        out, grad = p2(c)
        rows = pl.ds(pl.multiple_of(c * R, R), R)
        recv(out)
        value = r2f[c, 0, y]
        for d in range(1, Y):
            value = value + r2r[c, 0, d - 1].astype(F32)
        out_ref[rows, :] = value.astype(BF16)
        recv(grad)
        value = r2f[c, 1, z]
        for d in range(1, Z):
            value = value + r2r[c, 1, d - 1].astype(F32)
        grad_ref[rows, :] = value.astype(BF16)

    def tick(t, _):
        def when(c, stage):
            @pl.when((c >= 0) & (c < N))
            def _():
                stage(c)

        when(t + 2, lambda c: start(ag1(c)))
        when(t + 1, gather_on)
        when(t, forward)
        when(t, share)
        when(t - 1, activate)
        when(t - 2, pass_on)
        when(t - 2, backward)
        when(t - 3, narrow)
        when(t - 4, finish)
        return 0

    lax.fori_loop(0, N + 2, tick, 0)

    writes = []

    def weight_grad(staged, lhs, rhs, mask, hbm, n):
        high, wide = staged.shape

        def strip(i, _):
            rows = pl.ds(pl.multiple_of(i * BLOCK, BLOCK), BLOCK)
            left = lhs(rows)
            for at, width in column_tiles(wide):
                value = lax.dot_general(left, rhs(at, width), (((0,), (0,)), ((), ())), preferred_element_type=F32)
                for b in range(0, width, BLOCK):
                    kept = jnp.full((BLOCK, BLOCK), mask[i, (at + b) // BLOCK], jnp.int32).astype(F32)
                    staged[rows, at + b : at + b + BLOCK] = (value[:, b : b + BLOCK] * kept).astype(BF16)
            return 0

        lax.fori_loop(0, high // BLOCK, strip, 0)
        copy = pltpu.make_async_copy(staged, hbm, dw_sem.at[n])
        copy.start()
        writes.append(copy)

    everything = N * T

    def grads_of(j):
        return lambda at, width: hall[:, :, j, :, at : at + width].reshape(everything, width)

    def tokens_of(rows):
        return act[0, :, :, :, :, rows].reshape(everything, BLOCK)

    weight_grad(dg, tokens_of, grads_of(1), gate_mask, dgate_hbm, 0)
    weight_grad(du, tokens_of, grads_of(2), up_mask, dup_hbm, 1)
    narrow(N - 1)
    if N > 1:
        finish(N - 2)
    weight_grad(
        dd,
        lambda rows: hall[:, :, 0, :, rows].reshape(everything, BLOCK),
        lambda at, width: act[1, :, :, :, :, at : at + width].reshape(everything, width),
        down_mask,
        ddown_hbm,
        2,
    )
    finish(N - 1)

    def drain(c, _):
        for copies in (ag1(c), *ag2(c), [cx(c, j) for j in range(3)], rs(c), gx(c), [cf(c, d) for d in range(X)], *p1(c), *p2(c)):
            for copy in copies:
                copy.wait_send()
        return 0

    lax.fori_loop(0, N, drain, 0)
    for copy in writes:
        copy.wait()


def local(dims, tokens, cotangent, gate_weight, up_weight, down_weight, gate_mask, up_mask, down_mask):
    Z, Y, X, N, R = dims
    T = Z * Y * R
    DL, FL = gate_weight.shape
    half, Q = T // 2, T // 2 // X
    vmem, smem, hbm = (pl.BlockSpec(memory_space=s) for s in (pltpu.VMEM, pltpu.SMEM, pl.ANY))
    dma = pltpu.SemaphoreType.DMA
    zy = max(Z, Y)
    ax = max(zy - 1, 1)
    xx = max(X - 1, 1)
    return pl.pallas_call(
        functools.partial(kernel, dims),
        out_shape=(
            jax.ShapeDtypeStruct(tokens.shape, BF16),
            jax.ShapeDtypeStruct(tokens.shape, BF16),
            jax.ShapeDtypeStruct((DL, FL), BF16),
            jax.ShapeDtypeStruct((DL, FL), BF16),
            jax.ShapeDtypeStruct((FL, DL), BF16),
        ),
        in_specs=[vmem, vmem, hbm, hbm, hbm, smem, smem, smem],
        out_specs=(vmem, vmem, hbm, hbm, hbm),
        scratch_shapes=[
            pltpu.VMEM((DL, FL), BF16),
            pltpu.VMEM((DL, FL), BF16),
            pltpu.VMEM((FL, DL), BF16),
            pltpu.VMEM((2, N, Z, Y, R, DL), BF16),
            pltpu.VMEM((N, 3, T, FL), F32),
            pltpu.VMEM((N, 3, half, FL), F32),
            pltpu.VMEM((N, X, 3, Q, FL), BF16),
            pltpu.VMEM((N, xx, 3, Q, FL), BF16),
            pltpu.VMEM((N, 2 * X, 3, Q, FL), BF16),
            pltpu.VMEM((N, 2, Z, Y, R, DL), BF16),
            pltpu.VMEM((N, 2, ax, zy, R, DL), BF16),
            pltpu.VMEM((N, 2, zy, R, DL), F32),
            pltpu.VMEM((N, 2, zy, R, DL), BF16),
            pltpu.VMEM((N, 2, ax, R, DL), BF16),
            pltpu.VMEM((DL, FL), BF16),
            pltpu.VMEM((DL, FL), BF16),
            pltpu.VMEM((FL, DL), BF16),
            dma((3,)),
            dma((3,)),
            *[dma((N, 2, ax))] * 4,
            *[dma((N, 3))] * 2,
            *[dma((N, xx))] * 2,
            *[dma((N, xx))] * 2,
            *[dma((N, X))] * 2,
            *[dma((N, 2, ax))] * 4,
        ],
        compiler_params=pltpu.CompilerParams(
            collective_id=0, has_side_effects=True, vmem_limit_bytes=60 * 2**20
        ),
    )(tokens, cotangent, gate_weight, up_weight, down_weight, gate_mask, up_mask, down_mask)


def solution(mesh, dims=(4, 4, 4, 4, 16)):
    return jax.shard_map(
        functools.partial(local, dims),
        mesh=mesh,
        in_specs=(
            P("row", "col"),
            P("row", "col"),
            P("col", "row"),
            P("col", "row"),
            P("row", "col"),
            P("col", "row"),
            P("col", "row"),
            P("row", "col"),
        ),
        out_specs=(
            P("row", "col"),
            P("row", "col"),
            P("col", "row"),
            P("col", "row"),
            P("row", "col"),
        ),
        check_vma=False,
    )
```

```python
import functools

import jax
import jax.numpy as jnp
from jax import lax
from jax.experimental import pallas as pl
from jax.experimental.pallas import tpu as pltpu
from jax.sharding import PartitionSpec as P

BLOCK = 128
MESH = pl.DeviceIdType.MESH
F32 = jnp.float32
BF16 = jnp.bfloat16

ORDER = (
    ("gate_grads", ((0, 13),)),
    ("gather", ((2, 0), (3, 3))),
    ("forward", ((0, 1), (1, 2), (2, 3), (3, 5))),
    ("activate", ((0, 3), (1, 4), (2, 8), (3, 9))),
    ("gather_on", ((1, 0), (2, 1), (3, 3))),
    ("pass_on", ((0, 5), (1, 8), (2, 10), (3, 11))),
    ("relay", ((0, 2), (1, 3), (2, 6), (3, 7))),
    ("share", ((0, 1), (1, 2), (2, 3), (3, 5))),
    ("spread", ((0, 3), (1, 6), (2, 9), (3, 10))),
    ("narrow", ((0, 9), (1, 12), (2, 13), (3, 14))),
    ("up_grads", ((0, 12),)),
    ("down_grads", ((0, 14),)),
    ("backward", ((0, 6), (1, 9), (2, 10), (3, 11))),
    ("finish", ((0, 10), (1, 14), (2, 15), (3, 16))),
)
TICKS = 17


def column_tiles(width):
    return [(at, min(256, width - at)) for at in range(0, width, 256)]


def kernel(
    dims,
    tok_hbm, cot_hbm, gate_hbm, up_hbm, down_hbm, gate_mask, up_mask, down_mask,
    out_hbm, grad_hbm, dgate_hbm, dup_hbm, ddown_hbm,
    wg, wu, wd, act, part, rpart, xs, xq, xt, xr, hall, outp, r1, r2f, r2s, r2r, fin, dg, du, dd,
    own_sem, o_sem, w_sem, dw_sem, ag1_s, ag1_r, ag2_s, ag2_r, cx_s, cx_r, rs1_s, rs1_r, rs2_s, rs2_r, gx1_s, gx1_r, gx2_s, gx2_r, cf_s, cf_r,
    p1_s, p1_r, p2_s, p2_r,
):
    Z, Y, X, N, R = dims
    T = Z * Y * R
    half = T // 2
    Q = half // X
    H = Q // 2
    DL, FL = wg.shape
    row = lax.axis_index("row")
    col = lax.axis_index("col")
    z, y = row // Y, row % Y
    x, k = col // 2, col % 2

    def at_z(d):
        return (((z + d) % Z) * Y + y, col)

    def at_y(d):
        return (z * Y + (y + d) % Y, col)

    def at_x(d):
        return (row, ((x + d) % X) * 2 + k)

    other = (row, x * 2 + 1 - k)

    def remote(src, dst, ssem, rsem, where):
        return pltpu.make_async_remote_copy(
            src_ref=src, dst_ref=dst, send_sem=ssem, recv_sem=rsem, device_id=where, device_id_type=MESH
        )

    def ag1(c):
        return [
            remote(tok_hbm.at[c], act.at[0, c, z, y], ag1_s.at[c, 0, d - 1], ag1_r.at[c, 0, d - 1], at_y(d))
            for d in range(1, Y)
        ] + [
            remote(cot_hbm.at[c], act.at[1, c, z, y], ag1_s.at[c, 1, d - 1], ag1_r.at[c, 1, d - 1], at_z(d))
            for d in range(1, Z)
        ]

    def ag2(c):
        tok = [
            remote(act.at[0, c, z], act.at[0, c, z], ag2_s.at[c, 0, d - 1], ag2_r.at[c, 0, d - 1], at_z(d))
            for d in range(1, Z)
        ]
        cot = [
            remote(act.at[1, c, :, y], act.at[1, c, :, y], ag2_s.at[c, 1, d - 1], ag2_r.at[c, 1, d - 1], at_y(d))
            for d in range(1, Y)
        ]
        return tok, cot

    def cx(c, j):
        return remote(
            part.at[c, j, pl.ds((1 - k) * half, half)], rpart.at[c, j], cx_s.at[c, j], cx_r.at[c, j], other
        )

    def rs1(c):
        right, left, far = (x + 1) % X, (x + X - 1) % X, (x + 2) % X
        moves = (
            (xs.at[c, far, 0], xq.at[c, 0], 1),
            (xs.at[c, far, 1], xq.at[c, 1], X - 1),
            (xs.at[c, right, 1], xr.at[c, 0], 1),
            (xs.at[c, left, 0], xr.at[c, 1], X - 1),
        )
        return [remote(src, dst, rs1_s.at[c, i], rs1_r.at[c, i], at_x(d)) for i, (src, dst, d) in enumerate(moves)]

    def rs2(c):
        return [
            remote(xt.at[c, i], xr.at[c, 2 + i], rs2_s.at[c, i], rs2_r.at[c, i], at_x(d)) for i, d in ((0, 1), (1, X - 1))
        ]

    def gx1(c):
        mine = hall.at[c, k * X + x]
        return [remote(mine, mine, gx1_s.at[c, i], gx1_r.at[c, i], at_x(d)) for i, d in ((0, 1), (1, X - 1))]

    def gx2(c):
        copies = []
        for i, d in ((0, 1), (1, X - 1)):
            piece = hall.at[c, k * X + (x + X - d) % X, i]
            copies.append(remote(piece, piece, gx2_s.at[c, i], gx2_r.at[c, i], at_x(d)))
        return copies

    def cf(c, i):
        block = hall.at[c, k * X + (x + (0, X - 1, 1, 2)[i]) % X]
        return remote(block, block, cf_s.at[c, i], cf_r.at[c, i], other)

    def p1(c):
        out = [
            remote(outp.at[c, 0, (z + d) % Z], r1.at[c, 0, d - 1], p1_s.at[c, 0, d - 1], p1_r.at[c, 0, d - 1], at_z(d))
            for d in range(1, Z)
        ]
        grad = [
            remote(outp.at[c, 1, :, (y + d) % Y], r1.at[c, 1, d - 1], p1_s.at[c, 1, d - 1], p1_r.at[c, 1, d - 1], at_y(d))
            for d in range(1, Y)
        ]
        return out, grad

    def p2(c):
        out = [
            remote(r2s.at[c, 0, (y + d) % Y], r2r.at[c, 0, d - 1], p2_s.at[c, 0, d - 1], p2_r.at[c, 0, d - 1], at_y(d))
            for d in range(1, Y)
        ]
        grad = [
            remote(r2s.at[c, 1, (z + d) % Z], r2r.at[c, 1, d - 1], p2_s.at[c, 1, d - 1], p2_r.at[c, 1, d - 1], at_z(d))
            for d in range(1, Z)
        ]
        return out, grad

    def start(copies):
        for copy in copies:
            copy.start()

    def recv(copies):
        for copy in copies:
            copy.wait_recv()

    loads = [
        pltpu.make_async_copy(src, dst, w_sem.at[i])
        for i, (src, dst) in enumerate(((gate_hbm, wg), (up_hbm, wu), (down_hbm, wd)))
    ]
    own = [
        pltpu.make_async_copy(src, act.at[i, :, z, y], own_sem.at[i]) for i, src in enumerate((tok_hbm, cot_hbm))
    ]
    start(own)
    start(loads)
    peers = [other] + [at_x(d) for d in (1, X - 1)] + [at_y(d) for d in range(1, Y)] + [at_z(d) for d in range(1, Z)]
    barrier = pltpu.get_barrier_semaphore()
    for peer in peers:
        pl.semaphore_signal(barrier, inc=1, device_id=peer, device_id_type=MESH)
    pl.semaphore_wait(barrier, len(peers))

    def gather(c):
        start(ag1(c))

    def gather_on(c):
        recv(ag1(c))
        tok, cot = ag2(c)
        start(tok)
        start(cot)

    gather(0)
    gather(1)
    for copy in own:
        copy.wait()
    gather_on(0)

    for copy, weight, mask in zip(loads, (wg, wu, wd), (gate_mask, up_mask, down_mask)):
        copy.wait()
        high, wide = weight.shape[0] // BLOCK, weight.shape[1] // BLOCK

        def keep_row(i, _, weight=weight, mask=mask, wide=wide):
            rows = pl.ds(pl.multiple_of(i * BLOCK, BLOCK), BLOCK)
            for j in range(wide):
                cols = slice(j * BLOCK, (j + 1) * BLOCK)
                kept = jnp.full((BLOCK, BLOCK), mask[i, j], jnp.int32).astype(F32).astype(BF16)
                weight[rows, cols] = weight[rows, cols] * kept
            return 0

        lax.fori_loop(0, high, keep_row, 0)

    def forward(c):
        tok, cot = ag2(c)
        recv(tok)
        for j, weight in enumerate((wg, wu)):
            tokens = act[0, c].reshape(T, DL)
            for at, width in column_tiles(FL):
                part[c, j, :, at : at + width] = jnp.dot(
                    tokens, weight[:, at : at + width], preferred_element_type=F32
                )
            cx(c, j).start()
        recv(cot)
        upstream = act[1, c].reshape(T, DL)
        for at, width in column_tiles(FL):
            part[c, 2, :, at : at + width] = lax.dot_general(
                upstream, wd[at : at + width, :], (((1,), (1,)), ((), ())), preferred_element_type=F32
            )
        cx(c, 2).start()

    def mine(c, j, b, h):
        at = pl.multiple_of(b * Q + h * H, H)
        here = pl.ds(pl.multiple_of(k * half + at, H), H)
        return part[c, j, here, :] + rpart[c, j, pl.ds(at, H), :]

    def share(c):
        for j in range(3):
            cx(c, j).wait_recv()
            for b in range(X):
                for h in range(2):
                    xs[c, b, h, j] = mine(c, j, b, h).astype(BF16)
        start(rs1(c))

    def relay(c):
        arriving, onward = rs1(c), rs2(c)
        for i, d in ((0, 1), (1, X - 1)):
            arriving[i].wait_recv()
            for j in range(3):
                xt[c, i, j] = (mine(c, j, (x + d) % X, i) + xq[c, i, j].astype(F32)).astype(BF16)
            onward[i].start()

    def activate(c):
        recv(rs1(c)[2:])
        recv(rs2(c))
        block = k * X + x
        for h in range(2):

            def total(j, h=h):
                return mine(c, j, x, h) + xr[c, 1 - h, j].astype(F32) + xr[c, 2 + h, j].astype(F32)

            gate, up, back = total(0), total(1), total(2)
            s = 1.0 / (1.0 + jnp.exp(-gate))
            hall[c, block, h, 0] = (gate * s * up).astype(BF16)
            hall[c, block, h, 1] = (back * up * s * (1.0 + gate * (1.0 - s))).astype(BF16)
            hall[c, block, h, 2] = (back * gate * s).astype(BF16)
        start(gx1(c))
        cf(c, 0).start()

    def spread(c):
        for i, (arriving, onward) in enumerate(zip(gx1(c), gx2(c))):
            arriving.wait_recv()
            onward.start()
            cf(c, 1 + i).start()

    def pass_on(c):
        recv(gx2(c))
        cf(c, 3).start()

    def backward(c):
        for i in range(4):
            cf(c, i).wait_recv()
        out, grad = p1(c)
        hidden = hall[c, :, :, 0].reshape(T, FL)
        for at, width in column_tiles(DL):
            value = jnp.dot(hidden, wd[:, at : at + width], preferred_element_type=F32)
            outp[c, 0, :, :, :, at : at + width] = value.astype(BF16).reshape(Z, Y, R, width)
        start(out)
        grad_gate = hall[c, :, :, 1].reshape(T, FL)
        grad_up = hall[c, :, :, 2].reshape(T, FL)
        for at, width in column_tiles(DL):
            nt = (((1,), (1,)), ((), ()))
            value = lax.dot_general(grad_gate, wg[at : at + width, :], nt, preferred_element_type=F32)
            value += lax.dot_general(grad_up, wu[at : at + width, :], nt, preferred_element_type=F32)
            outp[c, 1, :, :, :, at : at + width] = value.astype(BF16).reshape(Z, Y, R, width)
        start(grad)

    def narrow(c):
        out, grad = p1(c)
        send_out, send_grad = p2(c)
        recv(out)
        for b in range(Y):
            value = outp[c, 0, z, b].astype(F32)
            for d in range(1, Z):
                value = value + r1[c, 0, d - 1, b].astype(F32)
            r2f[c, 0, b] = value
            r2s[c, 0, b] = value.astype(BF16)
        start(send_out)
        recv(grad)
        for b in range(Z):
            value = outp[c, 1, b, y].astype(F32)
            for d in range(1, Y):
                value = value + r1[c, 1, d - 1, b].astype(F32)
            r2f[c, 1, b] = value
            r2s[c, 1, b] = value.astype(BF16)
        start(send_grad)

    def final(c):
        return [
            pltpu.make_async_copy(fin.at[i, c], dst.at[c], o_sem.at[i, c]) for i, dst in enumerate((out_hbm, grad_hbm))
        ]

    def finish(c):
        out, grad = p2(c)
        recv(out)
        value = r2f[c, 0, y]
        for d in range(1, Y):
            value = value + r2r[c, 0, d - 1].astype(F32)
        fin[0, c] = value.astype(BF16)
        recv(grad)
        value = r2f[c, 1, z]
        for d in range(1, Z):
            value = value + r2r[c, 1, d - 1].astype(F32)
        fin[1, c] = value.astype(BF16)
        start(final(c))

    def weight_grad(staged, lhs, rhs, mask, hbm, n):
        high, wide = staged.shape
        for top, tall in column_tiles(high):
            left = lhs(top, tall)
            for at, width in column_tiles(wide):
                value = lax.dot_general(left, rhs(at, width), (((0,), (0,)), ((), ())), preferred_element_type=F32)
                for a in range(0, tall, BLOCK):
                    for b in range(0, width, BLOCK):
                        kept = jnp.full((BLOCK, BLOCK), mask[(top + a) // BLOCK, (at + b) // BLOCK], jnp.int32).astype(F32)
                        staged[top + a : top + a + BLOCK, at + b : at + b + BLOCK] = (
                            value[a : a + BLOCK, b : b + BLOCK] * kept
                        ).astype(BF16)
        pltpu.make_async_copy(staged, hbm, dw_sem.at[n]).start()

    everything = N * T

    def grads_of(j):
        return lambda at, width: hall[:, :, :, j, :, at : at + width].reshape(everything, width)

    def tokens_of(at, width):
        return act[0, :, :, :, :, at : at + width].reshape(everything, width)

    def upstream_of(at, width):
        return act[1, :, :, :, :, at : at + width].reshape(everything, width)

    def gate_grads(_):
        weight_grad(dg, tokens_of, grads_of(1), gate_mask, dgate_hbm, 0)

    def up_grads(_):
        weight_grad(du, tokens_of, grads_of(2), up_mask, dup_hbm, 1)

    def down_grads(_):
        weight_grad(dd, grads_of(0), upstream_of, down_mask, ddown_hbm, 2)

    stages = {
        "gather": gather, "gather_on": gather_on, "forward": forward, "share": share, "relay": relay,
        "activate": activate, "spread": spread, "pass_on": pass_on, "backward": backward, "narrow": narrow,
        "finish": finish, "gate_grads": gate_grads, "up_grads": up_grads, "down_grads": down_grads,
    }

    def tick(t, _):
        for name, ticks in ORDER:
            c, now = 0, False
            for n, at in ticks:
                c = c + n * (t == at).astype(jnp.int32)
                now = now | (t == at)

            @pl.when(now)
            def _(stage=stages[name], c=c):
                stage(c)

        return 0

    lax.fori_loop(0, TICKS, tick, 0)

    def drain(c, _):
        for copies in (ag1(c), *ag2(c), [cx(c, j) for j in range(3)], rs1(c), rs2(c), gx1(c), gx2(c)):
            for copy in copies:
                copy.wait_send()
        for copies in ([cf(c, i) for i in range(4)], *p1(c), *p2(c)):
            for copy in copies:
                copy.wait_send()
        for copy in final(c):
            copy.wait()
        return 0

    lax.fori_loop(0, N, drain, 0)
    for n, (staged, hbm) in enumerate(((dg, dgate_hbm), (du, dup_hbm), (dd, ddown_hbm))):
        pltpu.make_async_copy(staged, hbm, dw_sem.at[n]).wait()


PIECES = 4


def publish(*refs):
    ins, outs, held, in_sem, out_sem = refs[:5], refs[5:10], refs[10:15], refs[15], refs[16]
    arriving, leaving = [], []
    for i in (2, 3, 4, 0, 1):
        pieces = PIECES if i > 1 else 1
        rows = ins[i].shape[0] // pieces
        for n in range(pieces):
            at = pl.ds(n * rows, rows)
            arriving.append(pltpu.make_async_copy(ins[i].at[at], held[i].at[at], in_sem.at[i, n]))
            leaving.append(pltpu.make_async_copy(held[i].at[at], outs[i].at[at], out_sem.at[i, n]))
    for copy in arriving:
        copy.start()
    for come, go in zip(arriving, leaving):
        come.wait()
        go.start()
    for copy in leaving:
        copy.wait()


def local(dims, tokens, cotangent, gate_weight, up_weight, down_weight, gate_mask, up_mask, down_mask):
    Z, Y, X, N, R = dims
    T = Z * Y * R
    DL, FL = gate_weight.shape
    half, Q = T // 2, T // 2 // X
    H = Q // 2
    smem, hbm = (pl.BlockSpec(memory_space=s) for s in (pltpu.SMEM, pl.ANY))
    far = pl.BlockSpec(memory_space=pltpu.HBM)
    dma = pltpu.SemaphoreType.DMA
    zy = max(Z, Y)
    ax = max(zy - 1, 1)
    results = pl.pallas_call(
        functools.partial(kernel, dims),
        out_shape=(
            jax.ShapeDtypeStruct((N, R, DL), BF16),
            jax.ShapeDtypeStruct((N, R, DL), BF16),
            jax.ShapeDtypeStruct((DL, FL), BF16),
            jax.ShapeDtypeStruct((DL, FL), BF16),
            jax.ShapeDtypeStruct((FL, DL), BF16),
        ),
        in_specs=[hbm, hbm, hbm, hbm, hbm, smem, smem, smem],
        out_specs=(hbm,) * 5,
        scratch_shapes=[
            pltpu.VMEM((DL, FL), BF16),
            pltpu.VMEM((DL, FL), BF16),
            pltpu.VMEM((FL, DL), BF16),
            pltpu.VMEM((2, N, Z, Y, R, DL), BF16),
            pltpu.VMEM((N, 3, T, FL), F32),
            pltpu.VMEM((N, 3, half, FL), F32),
            pltpu.VMEM((N, X, 2, 3, H, FL), BF16),
            pltpu.VMEM((N, 2, 3, H, FL), BF16),
            pltpu.VMEM((N, 2, 3, H, FL), BF16),
            pltpu.VMEM((N, 4, 3, H, FL), BF16),
            pltpu.VMEM((N, 2 * X, 2, 3, H, FL), BF16),
            pltpu.VMEM((N, 2, Z, Y, R, DL), BF16),
            pltpu.VMEM((N, 2, ax, zy, R, DL), BF16),
            pltpu.VMEM((N, 2, zy, R, DL), F32),
            pltpu.VMEM((N, 2, zy, R, DL), BF16),
            pltpu.VMEM((N, 2, ax, R, DL), BF16),
            pltpu.VMEM((2, N, R, DL), BF16),
            pltpu.VMEM((DL, FL), BF16),
            pltpu.VMEM((DL, FL), BF16),
            pltpu.VMEM((FL, DL), BF16),
            dma((2,)),
            dma((2, N)),
            dma((3,)),
            dma((3,)),
            *[dma((N, 2, ax))] * 4,
            *[dma((N, 3))] * 2,
            *[dma((N, 4))] * 2,
            *[dma((N, 2))] * 6,
            *[dma((N, 4))] * 2,
            *[dma((N, 2, ax))] * 4,
        ],
        compiler_params=pltpu.CompilerParams(
            collective_id=0, has_side_effects=True, vmem_limit_bytes=60 * 2**20
        ),
    )(tokens.reshape(N, R, DL), cotangent.reshape(N, R, DL), gate_weight, up_weight, down_weight, gate_mask, up_mask, down_mask)
    shared = pl.pallas_call(
        publish,
        out_shape=tuple(jax.ShapeDtypeStruct(r.shape, r.dtype) for r in results),
        in_specs=[far] * 5,
        out_specs=(far,) * 5,
        scratch_shapes=[*[pltpu.VMEM(r.shape, r.dtype) for r in results], dma((5, PIECES)), dma((5, PIECES))],
        compiler_params=pltpu.CompilerParams(vmem_limit_bytes=60 * 2**20),
    )(*results)
    return (shared[0].reshape(tokens.shape), shared[1].reshape(tokens.shape), *shared[2:])


def solution(mesh, dims=(4, 4, 4, 4, 16)):
    return jax.shard_map(
        functools.partial(local, dims),
        mesh=mesh,
        in_specs=(
            P("row", "col"),
            P("row", "col"),
            P("col", "row"),
            P("col", "row"),
            P("row", "col"),
            P("col", "row"),
            P("col", "row"),
            P("row", "col"),
        ),
        out_specs=(
            P("row", "col"),
            P("row", "col"),
            P("col", "row"),
            P("col", "row"),
            P("row", "col"),
        ),
        check_vma=False,
    )
```

```python
import functools

import jax
import jax.numpy as jnp
from jax import lax
from jax.experimental import pallas as pl
from jax.experimental.pallas import tpu as pltpu
from jax.sharding import PartitionSpec as P

BLOCK = 128
MESH = pl.DeviceIdType.MESH
F32 = jnp.float32
BF16 = jnp.bfloat16

ORDER = (
    ("forward", 0, 0, (1, 4, 8, 9)),
    ("relay", 0, 0, (4, 7, 11, 13)),
    ("pass_on", 0, 0, (9, 14, 17, 19)),
    ("backward", 0, 0, (12, 14, 19, 20)),
    ("gate_grads", 1, 0, (23,)),
    ("forward", 1, 0, (2, 5, 7, 10)),
    ("down_grads", 1, 0, (20,)),
    ("gather", 0, 1, (0, 2, 3)),
    ("share", 1, 0, (3, 6, 8, 11)),
    ("narrow", 1, 0, (14, 15, 24, 25)),
    ("backward", 1, 0, (10, 13, 21, 22)),
    ("up_grads", 1, 0, (22,)),
    ("gather_on", 1, 0, (0, 2, 5, 6)),
    ("relay", 1, 0, (5, 7, 9, 13)),
    ("spread", 1, 0, (8, 10, 16, 18)),
    ("gate_grads", 0, 0, (22,)),
    ("spread", 0, 0, (8, 11, 14, 15)),
    ("activate", None, 0, (6, 8, 13, 14)),
    ("share", 0, 0, (2, 5, 8, 10)),
    ("gather_on", 0, 1, (1, 5, 7)),
    ("settle", None, 0, (8, 11, 14, 17)),
    ("down_grads", 0, 0, (22,)),
    ("narrow", 0, 0, (14, 16, 22, 23)),
    ("pass_on", 1, 0, (8, 12, 19, 20)),
    ("settle_on", None, 0, (12, 14, 25, 27)),
    ("gather", 1, 1, (0, 2, 4)),
    ("finish", 0, 0, (17, 19, 25, 26)),
    ("finish", 1, 0, (17, 18, 26, 27)),
    ("up_grads", 0, 0, (24,)),
)
TICKS = 28


def column_tiles(width):
    return [(at, min(256, width - at)) for at in range(0, width, 256)]


def kernel(
    dims,
    tok_hbm, cot_hbm, gate_hbm, up_hbm, down_hbm, gate_mask, up_mask, down_mask,
    out_hbm, grad_hbm, dgate_hbm, dup_hbm, ddown_hbm,
    wg, wu, wd, act, part, rpart, xs, xq, xt, xr, hall, outp, r1, r2f, r2s, r2r, fin, dg, du, dd,
    own_sem, o_sem, w_sem, dw_sem, ag1_s, ag1_r, ag2_s, ag2_r, cx_s, cx_r, rs1_s, rs1_r, rs2_s, rs2_r, gx1_s, gx1_r, gx2_s, gx2_r, cf_s, cf_r,
    p1_s, p1_r, p2_s, p2_r,
):
    Z, Y, X, N, R = dims
    T = Z * Y * R
    half = T // 2
    Q = half // X
    H = Q // 2
    DL, FL = wg.shape
    DH = DL // 2
    columns = (slice(0, DH), slice(DH, DL))
    row = lax.axis_index("row")
    col = lax.axis_index("col")
    z, y = row // Y, row % Y
    x, k = col // 2, col % 2

    def at_z(d):
        return (((z + d) % Z) * Y + y, col)

    def at_y(d):
        return (z * Y + (y + d) % Y, col)

    def at_x(d):
        return (row, ((x + d) % X) * 2 + k)

    other = (row, x * 2 + 1 - k)

    def remote(src, dst, ssem, rsem, where):
        return pltpu.make_async_remote_copy(
            src_ref=src, dst_ref=dst, send_sem=ssem, recv_sem=rsem, device_id=where, device_id_type=MESH
        )

    def ag1(c, g):
        return [
            remote(
                (tok_hbm, cot_hbm)[g].at[c, :, columns[h]], act.at[g, c, z, y, :, columns[h]],
                ag1_s.at[c, g, h, d - 1], ag1_r.at[c, g, h, d - 1], (at_y, at_z)[h](d),
            )
            for h, size in ((0, Y), (1, Z))
            for d in range(1, size)
        ]

    def ag2(c, g):
        pieces = (act.at[g, c, z, :, :, columns[0]], act.at[g, c, :, y, :, columns[1]])
        return [
            remote(pieces[h], pieces[h], ag2_s.at[c, g, h, d - 1], ag2_r.at[c, g, h, d - 1], (at_z, at_y)[h](d))
            for h, size in ((0, Z), (1, Y))
            for d in range(1, size)
        ]

    def cx(c, j):
        return remote(
            part.at[c, j, pl.ds((1 - k) * half, half)], rpart.at[c, j], cx_s.at[c, j], cx_r.at[c, j], other
        )

    def rs1(c, g):
        js = slice(0, 2) if g == 0 else slice(2, 3)
        right, left, far = (x + 1) % X, (x + X - 1) % X, (x + 2) % X
        moves = (
            (xs.at[c, far, 0, js], xq.at[c, 0, js], 1),
            (xs.at[c, far, 1, js], xq.at[c, 1, js], X - 1),
            (xs.at[c, right, 1, js], xr.at[c, 0, js], 1),
            (xs.at[c, left, 0, js], xr.at[c, 1, js], X - 1),
        )
        return [
            remote(src, dst, rs1_s.at[c, g, i], rs1_r.at[c, g, i], at_x(d)) for i, (src, dst, d) in enumerate(moves)
        ]

    def rs2(c, g):
        js = slice(0, 2) if g == 0 else slice(2, 3)
        return [
            remote(xt.at[c, i, js], xr.at[c, 2 + i, js], rs2_s.at[c, g, i], rs2_r.at[c, g, i], at_x(d))
            for i, d in ((0, 1), (1, X - 1))
        ]

    def gx1(c, g):
        js = slice(0, 1) if g == 0 else slice(1, 3)
        mine = hall.at[c, k * X + x, :, js]
        return [remote(mine, mine, gx1_s.at[c, g, i], gx1_r.at[c, g, i], at_x(d)) for i, d in ((0, 1), (1, X - 1))]

    def gx2(c, g):
        js = slice(0, 1) if g == 0 else slice(1, 3)
        pieces = [hall.at[c, k * X + (x + X - d) % X, i, js] for i, d in ((0, 1), (1, X - 1))]
        return [
            remote(pieces[i], pieces[i], gx2_s.at[c, g, i], gx2_r.at[c, g, i], at_x(d)) for i, d in ((0, 1), (1, X - 1))
        ]

    def cf(c, g, i):
        js = slice(0, 1) if g == 0 else slice(1, 3)
        block = hall.at[c, k * X + (x + (0, X - 1, 1, 2)[i]) % X, :, js]
        return remote(block, block, cf_s.at[c, g, i], cf_r.at[c, g, i], other)

    def p1(c, g, h):
        size, at = ((Z, at_z), (Y, at_y))[h]
        copies = []
        for d in range(1, size):
            piece = (outp.at[c, g, (z + d) % Z, :, :, columns[0]], outp.at[c, g, :, (y + d) % Y, :, columns[1]])[h]
            copies.append(remote(piece, r1.at[c, g, h, d - 1], p1_s.at[c, g, h, d - 1], p1_r.at[c, g, h, d - 1], at(d)))
        return copies

    def p2(c, g, h):
        size, at, me = ((Y, at_y, y), (Z, at_z, z))[h]
        return [
            remote(
                r2s.at[c, g, h, (me + d) % size], r2r.at[c, g, h, d - 1],
                p2_s.at[c, g, h, d - 1], p2_r.at[c, g, h, d - 1], at(d),
            )
            for d in range(1, size)
        ]

    def start(copies):
        for copy in copies:
            copy.start()

    def recv(copies):
        for copy in copies:
            copy.wait_recv()

    loads = [
        pltpu.make_async_copy(src, dst, w_sem.at[i])
        for i, (src, dst) in enumerate(((gate_hbm, wg), (up_hbm, wu), (down_hbm, wd)))
    ]
    own = [
        pltpu.make_async_copy(src, act.at[i, :, z, y], own_sem.at[i]) for i, src in enumerate((tok_hbm, cot_hbm))
    ]
    start(own)
    start(loads)
    peers = [other] + [at_x(d) for d in (1, X - 1)] + [at_y(d) for d in range(1, Y)] + [at_z(d) for d in range(1, Z)]
    barrier = pltpu.get_barrier_semaphore()
    for peer in peers:
        pl.semaphore_signal(barrier, inc=1, device_id=peer, device_id_type=MESH)
    pl.semaphore_wait(barrier, len(peers))

    def gather(c, g):
        start(ag1(c, g))

    def gather_on(c, g):
        recv(ag1(c, g))
        start(ag2(c, g))

    gather(0, 0)
    gather(0, 1)
    for copy in own:
        copy.wait()
    gather_on(0, 0)

    for copy, weight, mask in zip(loads, (wg, wu, wd), (gate_mask, up_mask, down_mask)):
        copy.wait()
        high, wide = weight.shape[0] // BLOCK, weight.shape[1] // BLOCK

        def keep_row(i, _, weight=weight, mask=mask, wide=wide):
            rows = pl.ds(pl.multiple_of(i * BLOCK, BLOCK), BLOCK)
            for j in range(wide):
                cols = slice(j * BLOCK, (j + 1) * BLOCK)
                kept = jnp.full((BLOCK, BLOCK), mask[i, j], jnp.int32).astype(F32).astype(BF16)
                weight[rows, cols] = weight[rows, cols] * kept
            return 0

        lax.fori_loop(0, high, keep_row, 0)

    def forward(c, g):
        recv(ag2(c, g))
        features = act[g, c].reshape(T, DL)
        for j in (0, 1) if g == 0 else (2,):
            for at, width in column_tiles(FL):
                if j < 2:
                    weight, sums = (wg, wu)[j][:, at : at + width], (((1,), (0,)), ((), ()))
                else:
                    weight, sums = wd[at : at + width, :], (((1,), (1,)), ((), ()))
                part[c, j, :, at : at + width] = lax.dot_general(features, weight, sums, preferred_element_type=F32)
            cx(c, j).start()

    def mine(c, j, b, h):
        at = pl.multiple_of(b * Q + h * H, H)
        here = pl.ds(pl.multiple_of(k * half + at, H), H)
        return part[c, j, here, :] + rpart[c, j, pl.ds(at, H), :]

    def share(c, g):
        for j in (0, 1) if g == 0 else (2,):
            cx(c, j).wait_recv()
            for b in range(X):
                for h in range(2):
                    xs[c, b, h, j] = mine(c, j, b, h).astype(BF16)
        start(rs1(c, g))

    def relay(c, g):
        arriving, onward = rs1(c, g), rs2(c, g)
        for i, d in ((0, 1), (1, X - 1)):
            arriving[i].wait_recv()
            for j in (0, 1) if g == 0 else (2,):
                xt[c, i, j] = (mine(c, j, (x + d) % X, i) + xq[c, i, j].astype(F32)).astype(BF16)
            onward[i].start()

    def activate(c):
        for g in range(2):
            recv(rs1(c, g)[2:])
            recv(rs2(c, g))
        block = k * X + x
        for h in range(2):

            def total(j, h=h):
                return mine(c, j, x, h) + xr[c, 1 - h, j].astype(F32) + xr[c, 2 + h, j].astype(F32)

            gate, up, back = total(0), total(1), total(2)
            s = 1.0 / (1.0 + jnp.exp(-gate))
            hall[c, block, h, 0] = (gate * s * up).astype(BF16)
            hall[c, block, h, 1] = (back * up * s * (1.0 + gate * (1.0 - s))).astype(BF16)
            hall[c, block, h, 2] = (back * gate * s).astype(BF16)
        for g in range(2):
            start(gx1(c, g))
            cf(c, g, 0).start()

    def spread(c, g):
        for i, (arriving, onward) in enumerate(zip(gx1(c, g), gx2(c, g))):
            arriving.wait_recv()
            onward.start()
            cf(c, g, 1 + i).start()

    def pass_on(c, g):
        recv(gx2(c, g))
        cf(c, g, 3).start()

    def backward(c, g):
        for i in range(4):
            cf(c, g, i).wait_recv()
        terms = ((0, wd),) if g == 0 else ((1, wg), (2, wu))
        for h in range(2):
            for at, width in column_tiles(DH):
                cols = slice(h * DH + at, h * DH + at + width)
                value = 0.0
                for j, weight in terms:
                    left = hall[c, :, :, j].reshape(T, FL)
                    if g == 0:
                        value += jnp.dot(left, weight[:, cols], preferred_element_type=F32)
                    else:
                        value += lax.dot_general(
                            left, weight[cols, :], (((1,), (1,)), ((), ())), preferred_element_type=F32
                        )
                outp[c, g, :, :, :, cols] = value.astype(BF16).reshape(Z, Y, R, width)
            start(p1(c, g, h))

    def narrow(c, g):
        for h, size, count in ((0, Z, Y), (1, Y, Z)):
            recv(p1(c, g, h))
            for b in range(count):
                value = (outp[c, g, z, b, :, columns[0]], outp[c, g, b, y, :, columns[1]])[h].astype(F32)
                for d in range(1, size):
                    value = value + r1[c, g, h, d - 1, b].astype(F32)
                r2f[c, g, h, b] = value
                r2s[c, g, h, b] = value.astype(BF16)
            start(p2(c, g, h))

    def final(c, g):
        return pltpu.make_async_copy(fin.at[g, c], (out_hbm, grad_hbm)[g].at[c], o_sem.at[g, c])

    def finish(c, g):
        for h, size, me in ((0, Y, y), (1, Z, z)):
            recv(p2(c, g, h))
            value = r2f[c, g, h, me]
            for d in range(1, size):
                value = value + r2r[c, g, h, d - 1].astype(F32)
            fin[g, c, :, columns[h]] = value.astype(BF16)
        final(c, g).start()

    def weight_write(staged, hbm, n, part_of):
        rows = slice(0, 512) if part_of == 0 else slice(512, staged.shape[0])
        return pltpu.make_async_copy(staged.at[rows], hbm.at[rows], dw_sem.at[n, part_of])

    def weight_grad(staged, lhs, rhs, mask, hbm, n, part_of):
        high, wide = staged.shape
        for top, tall in column_tiles(high)[2 * part_of : 2 * part_of + 2]:
            left = lhs(top, tall)
            for at, width in column_tiles(wide):
                value = lax.dot_general(left, rhs(at, width), (((0,), (0,)), ((), ())), preferred_element_type=F32)
                for a in range(0, tall, BLOCK):
                    for b in range(0, width, BLOCK):
                        kept = jnp.full((BLOCK, BLOCK), mask[(top + a) // BLOCK, (at + b) // BLOCK], jnp.int32).astype(F32)
                        staged[top + a : top + a + BLOCK, at + b : at + b + BLOCK] = (
                            value[a : a + BLOCK, b : b + BLOCK] * kept
                        ).astype(BF16)
        weight_write(staged, hbm, n, part_of).start()

    everything = N * T

    def grads_of(j):
        return lambda at, width: hall[:, :, :, j, :, at : at + width].reshape(everything, width)

    def tokens_of(at, width):
        return act[0, :, :, :, :, at : at + width].reshape(everything, width)

    def upstream_of(at, width):
        return act[1, :, :, :, :, at : at + width].reshape(everything, width)

    def gate_grads(_, part_of):
        weight_grad(dg, tokens_of, grads_of(1), gate_mask, dgate_hbm, 0, part_of)

    def up_grads(_, part_of):
        weight_grad(du, tokens_of, grads_of(2), up_mask, dup_hbm, 1, part_of)

    def down_grads(_, part_of):
        weight_grad(dd, grads_of(0), upstream_of, down_mask, ddown_hbm, 2, part_of)

    def sent(copies):
        for copy in copies:
            copy.wait_send()

    def settle(c):
        for g in range(2):
            sent(ag1(c, g) + ag2(c, g) + rs1(c, g) + rs2(c, g))
        sent([cx(c, j) for j in range(3)])

    def settle_on(c):
        for g in range(2):
            sent(gx1(c, g) + gx2(c, g) + [cf(c, g, i) for i in range(4)] + p1(c, g, 0) + p1(c, g, 1))

    stages = {
        "gather": gather, "gather_on": gather_on, "forward": forward, "share": share, "relay": relay,
        "activate": activate, "spread": spread, "pass_on": pass_on, "backward": backward, "narrow": narrow,
        "finish": finish, "gate_grads": gate_grads, "up_grads": up_grads, "down_grads": down_grads,
        "settle": settle, "settle_on": settle_on,
    }

    def tick(t, _):
        for name, group, first, ticks in ORDER:
            now = False
            for at in ticks:
                now = now | (t == at)

            @pl.when(now)
            def _(stage=stages[name], group=group, first=first, ticks=ticks):
                c = first
                for at in ticks[1:]:
                    c = c + (t >= at).astype(jnp.int32)
                if group is None:
                    stage(c)
                else:
                    stage(c, group)

        return 0

    lax.fori_loop(0, TICKS, tick, 0)

    def drain(c, _):
        for g in range(2):
            for h in range(2):
                sent(p2(c, g, h))
            final(c, g).wait()
        return 0

    lax.fori_loop(0, N, drain, 0)
    for n, (staged, hbm) in enumerate(((dg, dgate_hbm), (du, dup_hbm), (dd, ddown_hbm))):
        for part_of in range(2):
            weight_write(staged, hbm, n, part_of).wait()


PIECES = 4


def publish(*refs):
    ins, outs, held, in_sem, out_sem = refs[:5], refs[5:10], refs[10:15], refs[15], refs[16]
    arriving, leaving = [], []
    for i in (2, 3, 4, 0, 1):
        pieces = PIECES if i > 1 else 1
        rows = ins[i].shape[0] // pieces
        for n in range(pieces):
            at = pl.ds(n * rows, rows)
            arriving.append(pltpu.make_async_copy(ins[i].at[at], held[i].at[at], in_sem.at[i, n]))
            leaving.append(pltpu.make_async_copy(held[i].at[at], outs[i].at[at], out_sem.at[i, n]))
    for copy in arriving:
        copy.start()
    for come, go in zip(arriving, leaving):
        come.wait()
        go.start()
    for copy in leaving:
        copy.wait()


def local(dims, tokens, cotangent, gate_weight, up_weight, down_weight, gate_mask, up_mask, down_mask):
    Z, Y, X, N, R = dims
    T = Z * Y * R
    DL, FL = gate_weight.shape
    half, Q = T // 2, T // 2 // X
    H = Q // 2
    smem, hbm = (pl.BlockSpec(memory_space=s) for s in (pltpu.SMEM, pl.ANY))
    far = pl.BlockSpec(memory_space=pltpu.HBM)
    dma = pltpu.SemaphoreType.DMA
    zy = max(Z, Y)
    ax = max(zy - 1, 1)
    results = pl.pallas_call(
        functools.partial(kernel, dims),
        out_shape=(
            jax.ShapeDtypeStruct((N, R, DL), BF16),
            jax.ShapeDtypeStruct((N, R, DL), BF16),
            jax.ShapeDtypeStruct((DL, FL), BF16),
            jax.ShapeDtypeStruct((DL, FL), BF16),
            jax.ShapeDtypeStruct((FL, DL), BF16),
        ),
        in_specs=[hbm, hbm, hbm, hbm, hbm, smem, smem, smem],
        out_specs=(hbm,) * 5,
        scratch_shapes=[
            pltpu.VMEM((DL, FL), BF16),
            pltpu.VMEM((DL, FL), BF16),
            pltpu.VMEM((FL, DL), BF16),
            pltpu.VMEM((2, N, Z, Y, R, DL), BF16),
            pltpu.VMEM((N, 3, T, FL), F32),
            pltpu.VMEM((N, 3, half, FL), F32),
            pltpu.VMEM((N, X, 2, 3, H, FL), BF16),
            pltpu.VMEM((N, 2, 3, H, FL), BF16),
            pltpu.VMEM((N, 2, 3, H, FL), BF16),
            pltpu.VMEM((N, 4, 3, H, FL), BF16),
            pltpu.VMEM((N, 2 * X, 2, 3, H, FL), BF16),
            pltpu.VMEM((N, 2, Z, Y, R, DL), BF16),
            pltpu.VMEM((N, 2, 2, ax, zy, R, DL // 2), BF16),
            pltpu.VMEM((N, 2, 2, zy, R, DL // 2), F32),
            pltpu.VMEM((N, 2, 2, zy, R, DL // 2), BF16),
            pltpu.VMEM((N, 2, 2, ax, R, DL // 2), BF16),
            pltpu.VMEM((2, N, R, DL), BF16),
            pltpu.VMEM((DL, FL), BF16),
            pltpu.VMEM((DL, FL), BF16),
            pltpu.VMEM((FL, DL), BF16),
            dma((2,)),
            dma((2, N)),
            dma((3,)),
            dma((3, 2)),
            *[dma((N, 2, 2, ax))] * 4,
            *[dma((N, 3))] * 2,
            *[dma((N, 2, 4))] * 2,
            *[dma((N, 2, 2))] * 6,
            *[dma((N, 2, 4))] * 2,
            *[dma((N, 2, 2, ax))] * 4,
        ],
        compiler_params=pltpu.CompilerParams(
            collective_id=0, has_side_effects=True, vmem_limit_bytes=60 * 2**20
        ),
    )(tokens.reshape(N, R, DL), cotangent.reshape(N, R, DL), gate_weight, up_weight, down_weight, gate_mask, up_mask, down_mask)
    shared = pl.pallas_call(
        publish,
        out_shape=tuple(jax.ShapeDtypeStruct(r.shape, r.dtype) for r in results),
        in_specs=[far] * 5,
        out_specs=(far,) * 5,
        scratch_shapes=[*[pltpu.VMEM(r.shape, r.dtype) for r in results], dma((5, PIECES)), dma((5, PIECES))],
        compiler_params=pltpu.CompilerParams(vmem_limit_bytes=60 * 2**20),
    )(*results)
    return (shared[0].reshape(tokens.shape), shared[1].reshape(tokens.shape), *shared[2:])


def solution(mesh, dims=(4, 4, 4, 4, 16)):
    return jax.shard_map(
        functools.partial(local, dims),
        mesh=mesh,
        in_specs=(
            P("row", "col"),
            P("row", "col"),
            P("col", "row"),
            P("col", "row"),
            P("row", "col"),
            P("col", "row"),
            P("col", "row"),
            P("row", "col"),
        ),
        out_specs=(
            P("row", "col"),
            P("row", "col"),
            P("col", "row"),
            P("col", "row"),
            P("row", "col"),
        ),
        check_vma=False,
    )
```

```python
import functools

import jax
import jax.numpy as jnp
from jax import lax
from jax.experimental import pallas as pl
from jax.experimental.pallas import tpu as pltpu
from jax.sharding import PartitionSpec as P

BLOCK = 128
MESH = pl.DeviceIdType.MESH
F32 = jnp.float32
BF16 = jnp.bfloat16

ORDER = (
    ("gather_on", 1, 0, (1, 2, 4, 6)),
    ("settle", None, 0, (9, 12, 16, 17)),
    ("spread", 0, 0, (10, 12, 15, 16)),
    ("gate_grads", 1, 0, (23,)),
    ("share", 1, 0, (2, 4, 10, 11)),
    ("up_grads", 0, 0, (22,)),
    ("spread", 1, 0, (9, 12, 15, 17)),
    ("gather", 1, 1, (1, 2, 3)),
    ("gather", 0, 1, (0, 1, 2)),
    ("down_grads", 1, 0, (22,)),
    ("narrow", 0, 0, (14, 18, 22, 23)),
    ("forward", 0, 0, (1, 3, 5, 10)),
    ("backward", 0, 0, (12, 14, 19, 20)),
    ("relay", 0, 0, (3, 7, 11, 12)),
    ("gather_on", 0, 1, (1, 3, 4)),
    ("pass_on", 0, 0, (11, 13, 17, 19)),
    ("narrow", 1, 0, (13, 18, 24, 25)),
    ("down_grads", 0, 0, (25,)),
    ("gate_grads", 0, 0, (22,)),
    ("up_grads", 1, 0, (25,)),
    ("relay", 1, 0, (3, 6, 11, 12)),
    ("forward", 1, 0, (1, 3, 8, 10)),
    ("settle_on", None, 0, (12, 19, 24, 25)),
    ("activate", None, 0, (4, 10, 12, 14)),
    ("pass_on", 1, 0, (10, 13, 18, 20)),
    ("share", 0, 0, (1, 3, 7, 10)),
    ("backward", 1, 0, (10, 14, 20, 21)),
    ("finish", 0, 0, (18, 23, 25, 26)),
    ("finish", 1, 0, (17, 21, 25, 26)),
)
TICKS = 27


def column_tiles(width):
    return [(at, min(256, width - at)) for at in range(0, width, 256)]


def kernel(
    dims,
    tok_hbm, cot_hbm, gate_hbm, up_hbm, down_hbm, gate_mask, up_mask, down_mask,
    out_hbm, grad_hbm, dgate_hbm, dup_hbm, ddown_hbm,
    wg, wu, wd, act, part, rpart, xs, xq, xt, xr, hall, outp, r1, r2f, r2s, r2r, fin, dg, du, dd,
    own_sem, o_sem, w_sem, dw_sem, ag1_s, ag1_r, ag2_s, ag2_r, cx_s, cx_r, rs1_s, rs1_r, rs2_s, rs2_r, gx1_s, gx1_r, gx2_s, gx2_r, cf_s, cf_r,
    p1_s, p1_r, p2_s, p2_r,
):
    Z, Y, X, N, R = dims
    T = Z * Y * R
    half = T // 2
    Q = half // X
    H = Q // 2
    DL, FL = wg.shape
    DH = DL // 2
    columns = (slice(0, DH), slice(DH, DL))
    row = lax.axis_index("row")
    col = lax.axis_index("col")
    z, y = row // Y, row % Y
    x, k = col // 2, col % 2

    def at_z(d):
        return (((z + d) % Z) * Y + y, col)

    def at_y(d):
        return (z * Y + (y + d) % Y, col)

    def at_x(d):
        return (row, ((x + d) % X) * 2 + k)

    other = (row, x * 2 + 1 - k)

    def remote(src, dst, ssem, rsem, where):
        return pltpu.make_async_remote_copy(
            src_ref=src, dst_ref=dst, send_sem=ssem, recv_sem=rsem, device_id=where, device_id_type=MESH
        )

    def ag1(c, g):
        return [
            remote(
                (tok_hbm, cot_hbm)[g].at[c, :, columns[h]], act.at[g, c, z, y, :, columns[h]],
                ag1_s.at[c, g, h, d - 1], ag1_r.at[c, g, h, d - 1], (at_y, at_z)[h](d),
            )
            for h, size in ((0, Y), (1, Z))
            for d in range(1, size)
        ]

    def ag2(c, g):
        pieces = (act.at[g, c, z, :, :, columns[0]], act.at[g, c, :, y, :, columns[1]])
        return [
            remote(pieces[h], pieces[h], ag2_s.at[c, g, h, d - 1], ag2_r.at[c, g, h, d - 1], (at_z, at_y)[h](d))
            for h, size in ((0, Z), (1, Y))
            for d in range(1, size)
        ]

    def cx(c, j):
        return remote(
            part.at[c, j, pl.ds((1 - k) * half, half)], rpart.at[c, j], cx_s.at[c, j], cx_r.at[c, j], other
        )

    def rs1(c, g):
        js = slice(0, 2) if g == 0 else slice(2, 3)
        right, left, far = (x + 1) % X, (x + X - 1) % X, (x + 2) % X
        moves = (
            (xs.at[c, far, 0, js], xq.at[c, 0, js], 1),
            (xs.at[c, far, 1, js], xq.at[c, 1, js], X - 1),
            (xs.at[c, right, 1, js], xr.at[c, 0, js], 1),
            (xs.at[c, left, 0, js], xr.at[c, 1, js], X - 1),
        )
        return [
            remote(src, dst, rs1_s.at[c, g, i], rs1_r.at[c, g, i], at_x(d)) for i, (src, dst, d) in enumerate(moves)
        ]

    def rs2(c, g):
        js = slice(0, 2) if g == 0 else slice(2, 3)
        return [
            remote(xt.at[c, i, js], xr.at[c, 2 + i, js], rs2_s.at[c, g, i], rs2_r.at[c, g, i], at_x(d))
            for i, d in ((0, 1), (1, X - 1))
        ]

    def gx1(c, g):
        js = slice(0, 1) if g == 0 else slice(1, 3)
        mine = hall.at[c, k * X + x, :, js]
        return [remote(mine, mine, gx1_s.at[c, g, i], gx1_r.at[c, g, i], at_x(d)) for i, d in ((0, 1), (1, X - 1))]

    def gx2(c, g):
        js = slice(0, 1) if g == 0 else slice(1, 3)
        pieces = [hall.at[c, k * X + (x + X - d) % X, i, js] for i, d in ((0, 1), (1, X - 1))]
        return [
            remote(pieces[i], pieces[i], gx2_s.at[c, g, i], gx2_r.at[c, g, i], at_x(d)) for i, d in ((0, 1), (1, X - 1))
        ]

    def cf(c, g, i):
        js = slice(0, 1) if g == 0 else slice(1, 3)
        block = hall.at[c, k * X + (x + (0, X - 1, 1, 2)[i]) % X, :, js]
        return remote(block, block, cf_s.at[c, g, i], cf_r.at[c, g, i], other)

    def p1(c, g, h):
        size, at = ((Z, at_z), (Y, at_y))[h]
        copies = []
        for d in range(1, size):
            piece = (outp.at[c, g, (z + d) % Z, :, :, columns[0]], outp.at[c, g, :, (y + d) % Y, :, columns[1]])[h]
            copies.append(remote(piece, r1.at[c, g, h, d - 1], p1_s.at[c, g, h, d - 1], p1_r.at[c, g, h, d - 1], at(d)))
        return copies

    def p2(c, g, h):
        size, at, me = ((Y, at_y, y), (Z, at_z, z))[h]
        return [
            remote(
                r2s.at[c, g, h, (me + d) % size], r2r.at[c, g, h, d - 1],
                p2_s.at[c, g, h, d - 1], p2_r.at[c, g, h, d - 1], at(d),
            )
            for d in range(1, size)
        ]

    def start(copies):
        for copy in copies:
            copy.start()

    def recv(copies):
        for copy in copies:
            copy.wait_recv()

    loads = [
        pltpu.make_async_copy(src, dst, w_sem.at[i])
        for i, (src, dst) in enumerate(((gate_hbm, wg), (up_hbm, wu), (down_hbm, wd)))
    ]
    own = [
        pltpu.make_async_copy(src, act.at[i, :, z, y], own_sem.at[i]) for i, src in enumerate((tok_hbm, cot_hbm))
    ]
    start(own)
    start(loads)
    peers = [other] + [at_x(d) for d in (1, X - 1)] + [at_y(d) for d in range(1, Y)] + [at_z(d) for d in range(1, Z)]
    barrier = pltpu.get_barrier_semaphore()
    for peer in peers:
        pl.semaphore_signal(barrier, inc=1, device_id=peer, device_id_type=MESH)
    pl.semaphore_wait(barrier, len(peers))

    def gather(c, g):
        start(ag1(c, g))

    def gather_on(c, g):
        recv(ag1(c, g))
        start(ag2(c, g))

    gather(0, 0)
    gather(0, 1)
    for copy in own:
        copy.wait()
    gather_on(0, 0)

    for copy, weight, mask in zip(loads, (wg, wu, wd), (gate_mask, up_mask, down_mask)):
        copy.wait()
        high, wide = weight.shape[0] // BLOCK, weight.shape[1] // BLOCK

        def keep_row(i, _, weight=weight, mask=mask, wide=wide):
            rows = pl.ds(pl.multiple_of(i * BLOCK, BLOCK), BLOCK)
            for j in range(wide):
                cols = slice(j * BLOCK, (j + 1) * BLOCK)
                kept = jnp.full((BLOCK, BLOCK), mask[i, j], jnp.int32).astype(F32).astype(BF16)
                weight[rows, cols] = weight[rows, cols] * kept
            return 0

        lax.fori_loop(0, high, keep_row, 0)

    def forward(c, g):
        recv(ag2(c, g))
        features = act[g, c].reshape(T, DL)
        for j in (0, 1) if g == 0 else (2,):
            for at, width in column_tiles(FL):
                if j < 2:
                    weight, sums = (wg, wu)[j][:, at : at + width], (((1,), (0,)), ((), ()))
                else:
                    weight, sums = wd[at : at + width, :], (((1,), (1,)), ((), ()))
                part[c, j, :, at : at + width] = lax.dot_general(features, weight, sums, preferred_element_type=F32)
            cx(c, j).start()

    def mine(c, j, b, h):
        at = pl.multiple_of(b * Q + h * H, H)
        here = pl.ds(pl.multiple_of(k * half + at, H), H)
        return part[c, j, here, :] + rpart[c, j, pl.ds(at, H), :]

    def share(c, g):
        for j in (0, 1) if g == 0 else (2,):
            cx(c, j).wait_recv()
            for b in range(X):
                for h in range(2):
                    xs[c, b, h, j] = mine(c, j, b, h).astype(BF16)
        start(rs1(c, g))

    def relay(c, g):
        arriving, onward = rs1(c, g), rs2(c, g)
        for i, d in ((0, 1), (1, X - 1)):
            arriving[i].wait_recv()
            for j in (0, 1) if g == 0 else (2,):
                xt[c, i, j] = (mine(c, j, (x + d) % X, i) + xq[c, i, j].astype(F32)).astype(BF16)
            onward[i].start()

    def activate(c):
        for g in range(2):
            recv(rs1(c, g)[2:])
            recv(rs2(c, g))
        block = k * X + x
        for h in range(2):

            def total(j, h=h):
                return mine(c, j, x, h) + xr[c, 1 - h, j].astype(F32) + xr[c, 2 + h, j].astype(F32)

            gate, up, back = total(0), total(1), total(2)
            s = 1.0 / (1.0 + jnp.exp(-gate))
            hall[c, block, h, 0] = (gate * s * up).astype(BF16)
            hall[c, block, h, 1] = (back * up * s * (1.0 + gate * (1.0 - s))).astype(BF16)
            hall[c, block, h, 2] = (back * gate * s).astype(BF16)
        for g in range(2):
            start(gx1(c, g))
            cf(c, g, 0).start()

    def spread(c, g):
        for i, (arriving, onward) in enumerate(zip(gx1(c, g), gx2(c, g))):
            arriving.wait_recv()
            onward.start()
            cf(c, g, 1 + i).start()

    def pass_on(c, g):
        recv(gx2(c, g))
        cf(c, g, 3).start()

    def backward(c, g):
        for i in range(4):
            cf(c, g, i).wait_recv()
        terms = ((0, wd),) if g == 0 else ((1, wg), (2, wu))
        for h in range(2):
            for at, width in column_tiles(DH):
                cols = slice(h * DH + at, h * DH + at + width)
                value = 0.0
                for j, weight in terms:
                    left = hall[c, :, :, j].reshape(T, FL)
                    if g == 0:
                        value += jnp.dot(left, weight[:, cols], preferred_element_type=F32)
                    else:
                        value += lax.dot_general(
                            left, weight[cols, :], (((1,), (1,)), ((), ())), preferred_element_type=F32
                        )
                outp[c, g, :, :, :, cols] = value.astype(BF16).reshape(Z, Y, R, width)
            start(p1(c, g, h))

    def narrow(c, g):
        for h, size, count in ((0, Z, Y), (1, Y, Z)):
            recv(p1(c, g, h))
            for b in range(count):
                value = (outp[c, g, z, b, :, columns[0]], outp[c, g, b, y, :, columns[1]])[h].astype(F32)
                for d in range(1, size):
                    value = value + r1[c, g, h, d - 1, b].astype(F32)
                r2f[c, g, h, b] = value
                r2s[c, g, h, b] = value.astype(BF16)
            start(p2(c, g, h))

    def final(c, g):
        return pltpu.make_async_copy(fin.at[g, c], (out_hbm, grad_hbm)[g].at[c], o_sem.at[g, c])

    def finish(c, g):
        for h, size, me in ((0, Y, y), (1, Z, z)):
            recv(p2(c, g, h))
            value = r2f[c, g, h, me]
            for d in range(1, size):
                value = value + r2r[c, g, h, d - 1].astype(F32)
            fin[g, c, :, columns[h]] = value.astype(BF16)
        final(c, g).start()

    def weight_write(staged, hbm, n, part_of):
        rows = slice(0, 512) if part_of == 0 else slice(512, staged.shape[0])
        return pltpu.make_async_copy(staged.at[rows], hbm.at[rows], dw_sem.at[n, part_of])

    def weight_grad(staged, lhs, rhs, mask, hbm, n, part_of):
        high, wide = staged.shape
        for top, tall in column_tiles(high)[2 * part_of : 2 * part_of + 2]:
            left = lhs(top, tall)
            for at, width in column_tiles(wide):
                value = lax.dot_general(left, rhs(at, width), (((0,), (0,)), ((), ())), preferred_element_type=F32)
                for a in range(0, tall, BLOCK):
                    for b in range(0, width, BLOCK):
                        kept = jnp.full((BLOCK, BLOCK), mask[(top + a) // BLOCK, (at + b) // BLOCK], jnp.int32).astype(F32)
                        staged[top + a : top + a + BLOCK, at + b : at + b + BLOCK] = (
                            value[a : a + BLOCK, b : b + BLOCK] * kept
                        ).astype(BF16)
        weight_write(staged, hbm, n, part_of).start()

    everything = N * T

    def grads_of(j):
        return lambda at, width: hall[:, :, :, j, :, at : at + width].reshape(everything, width)

    def tokens_of(at, width):
        return act[0, :, :, :, :, at : at + width].reshape(everything, width)

    def upstream_of(at, width):
        return act[1, :, :, :, :, at : at + width].reshape(everything, width)

    def gate_grads(_, part_of):
        weight_grad(dg, tokens_of, grads_of(1), gate_mask, dgate_hbm, 0, part_of)

    def up_grads(_, part_of):
        weight_grad(du, tokens_of, grads_of(2), up_mask, dup_hbm, 1, part_of)

    def down_grads(_, part_of):
        weight_grad(dd, grads_of(0), upstream_of, down_mask, ddown_hbm, 2, part_of)

    def sent(copies):
        for copy in copies:
            copy.wait_send()

    def settle(c):
        for g in range(2):
            sent(ag1(c, g) + ag2(c, g) + rs1(c, g) + rs2(c, g))
        sent([cx(c, j) for j in range(3)])

    def settle_on(c):
        for g in range(2):
            sent(gx1(c, g) + gx2(c, g) + [cf(c, g, i) for i in range(4)] + p1(c, g, 0) + p1(c, g, 1))

    stages = {
        "gather": gather, "gather_on": gather_on, "forward": forward, "share": share, "relay": relay,
        "activate": activate, "spread": spread, "pass_on": pass_on, "backward": backward, "narrow": narrow,
        "finish": finish, "gate_grads": gate_grads, "up_grads": up_grads, "down_grads": down_grads,
        "settle": settle, "settle_on": settle_on,
    }

    def tick(t, _):
        for name, group, first, ticks in ORDER:
            now = False
            for at in ticks:
                now = now | (t == at)

            @pl.when(now)
            def _(stage=stages[name], group=group, first=first, ticks=ticks):
                c = first
                for at in ticks[1:]:
                    c = c + (t >= at).astype(jnp.int32)
                if group is None:
                    stage(c)
                else:
                    stage(c, group)

        return 0

    lax.fori_loop(0, TICKS, tick, 0)

    def drain(c, _):
        for g in range(2):
            for h in range(2):
                sent(p2(c, g, h))
            final(c, g).wait()
        return 0

    lax.fori_loop(0, N, drain, 0)
    for n, (staged, hbm) in enumerate(((dg, dgate_hbm), (du, dup_hbm), (dd, ddown_hbm))):
        for part_of in range(2):
            weight_write(staged, hbm, n, part_of).wait()


PIECES = 4


def publish(*refs):
    ins, outs, held, in_sem, out_sem = refs[:5], refs[5:10], refs[10:15], refs[15], refs[16]
    arriving, leaving = [], []
    for i in (2, 3, 4, 0, 1):
        pieces = PIECES if i > 1 else 1
        rows = ins[i].shape[0] // pieces
        for n in range(pieces):
            at = pl.ds(n * rows, rows)
            arriving.append(pltpu.make_async_copy(ins[i].at[at], held[i].at[at], in_sem.at[i, n]))
            leaving.append(pltpu.make_async_copy(held[i].at[at], outs[i].at[at], out_sem.at[i, n]))
    for copy in arriving:
        copy.start()
    for come, go in zip(arriving, leaving):
        come.wait()
        go.start()
    for copy in leaving:
        copy.wait()


def local(dims, tokens, cotangent, gate_weight, up_weight, down_weight, gate_mask, up_mask, down_mask):
    Z, Y, X, N, R = dims
    T = Z * Y * R
    DL, FL = gate_weight.shape
    half, Q = T // 2, T // 2 // X
    H = Q // 2
    smem, hbm = (pl.BlockSpec(memory_space=s) for s in (pltpu.SMEM, pl.ANY))
    far = pl.BlockSpec(memory_space=pltpu.HBM)
    dma = pltpu.SemaphoreType.DMA
    zy = max(Z, Y)
    ax = max(zy - 1, 1)
    results = pl.pallas_call(
        functools.partial(kernel, dims),
        out_shape=(
            jax.ShapeDtypeStruct((N, R, DL), BF16),
            jax.ShapeDtypeStruct((N, R, DL), BF16),
            jax.ShapeDtypeStruct((DL, FL), BF16),
            jax.ShapeDtypeStruct((DL, FL), BF16),
            jax.ShapeDtypeStruct((FL, DL), BF16),
        ),
        in_specs=[hbm, hbm, hbm, hbm, hbm, smem, smem, smem],
        out_specs=(hbm,) * 5,
        scratch_shapes=[
            pltpu.VMEM((DL, FL), BF16),
            pltpu.VMEM((DL, FL), BF16),
            pltpu.VMEM((FL, DL), BF16),
            pltpu.VMEM((2, N, Z, Y, R, DL), BF16),
            pltpu.VMEM((N, 3, T, FL), F32),
            pltpu.VMEM((N, 3, half, FL), F32),
            pltpu.VMEM((N, X, 2, 3, H, FL), BF16),
            pltpu.VMEM((N, 2, 3, H, FL), BF16),
            pltpu.VMEM((N, 2, 3, H, FL), BF16),
            pltpu.VMEM((N, 4, 3, H, FL), BF16),
            pltpu.VMEM((N, 2 * X, 2, 3, H, FL), BF16),
            pltpu.VMEM((N, 2, Z, Y, R, DL), BF16),
            pltpu.VMEM((N, 2, 2, ax, zy, R, DL // 2), BF16),
            pltpu.VMEM((N, 2, 2, zy, R, DL // 2), F32),
            pltpu.VMEM((N, 2, 2, zy, R, DL // 2), BF16),
            pltpu.VMEM((N, 2, 2, ax, R, DL // 2), BF16),
            pltpu.VMEM((2, N, R, DL), BF16),
            pltpu.VMEM((DL, FL), BF16),
            pltpu.VMEM((DL, FL), BF16),
            pltpu.VMEM((FL, DL), BF16),
            dma((2,)),
            dma((2, N)),
            dma((3,)),
            dma((3, 2)),
            *[dma((N, 2, 2, ax))] * 4,
            *[dma((N, 3))] * 2,
            *[dma((N, 2, 4))] * 2,
            *[dma((N, 2, 2))] * 6,
            *[dma((N, 2, 4))] * 2,
            *[dma((N, 2, 2, ax))] * 4,
        ],
        compiler_params=pltpu.CompilerParams(
            collective_id=0, has_side_effects=True, vmem_limit_bytes=60 * 2**20
        ),
    )(tokens.reshape(N, R, DL), cotangent.reshape(N, R, DL), gate_weight, up_weight, down_weight, gate_mask, up_mask, down_mask)
    shared = pl.pallas_call(
        publish,
        out_shape=tuple(jax.ShapeDtypeStruct(r.shape, r.dtype) for r in results),
        in_specs=[far] * 5,
        out_specs=(far,) * 5,
        scratch_shapes=[*[pltpu.VMEM(r.shape, r.dtype) for r in results], dma((5, PIECES)), dma((5, PIECES))],
        compiler_params=pltpu.CompilerParams(vmem_limit_bytes=60 * 2**20),
    )(*results)
    return (shared[0].reshape(tokens.shape), shared[1].reshape(tokens.shape), *shared[2:])


def solution(mesh, dims=(4, 4, 4, 4, 16)):
    return jax.shard_map(
        functools.partial(local, dims),
        mesh=mesh,
        in_specs=(
            P("row", "col"),
            P("row", "col"),
            P("col", "row"),
            P("col", "row"),
            P("row", "col"),
            P("col", "row"),
            P("col", "row"),
            P("row", "col"),
        ),
        out_specs=(
            P("row", "col"),
            P("row", "col"),
            P("col", "row"),
            P("col", "row"),
            P("row", "col"),
        ),
        check_vma=False,
    )
```

```python
import functools

import jax
import jax.numpy as jnp
from jax import lax
from jax.experimental import pallas as pl
from jax.experimental.pallas import tpu as pltpu
from jax.sharding import PartitionSpec as P

BLOCK = 128
MESH = pl.DeviceIdType.MESH
F32 = jnp.float32
BF16 = jnp.bfloat16

ORDER = (
    ("gather_on", 1, 0, (1, 2, 4, 6)),
    ("settle", None, 0, (9, 12, 16, 17)),
    ("spread", 0, 0, (10, 12, 15, 16)),
    ("gate_grads", 1, 0, (23,)),
    ("share", 1, 0, (2, 4, 10, 11)),
    ("up_grads", 0, 0, (22,)),
    ("spread", 1, 0, (9, 12, 15, 17)),
    ("gather", 1, 1, (1, 2, 3)),
    ("gather", 0, 1, (0, 1, 2)),
    ("down_grads", 1, 0, (22,)),
    ("narrow", 0, 0, (14, 18, 22, 23)),
    ("forward", 0, 0, (1, 3, 5, 10)),
    ("backward", 0, 0, (12, 14, 19, 20)),
    ("relay", 0, 0, (3, 7, 11, 12)),
    ("gather_on", 0, 1, (1, 3, 4)),
    ("pass_on", 0, 0, (11, 13, 17, 19)),
    ("narrow", 1, 0, (13, 18, 24, 25)),
    ("down_grads", 0, 0, (25,)),
    ("gate_grads", 0, 0, (22,)),
    ("up_grads", 1, 0, (25,)),
    ("relay", 1, 0, (3, 6, 11, 12)),
    ("forward", 1, 0, (1, 3, 8, 10)),
    ("settle_on", None, 0, (12, 19, 24, 25)),
    ("activate", None, 0, (4, 10, 12, 14)),
    ("pass_on", 1, 0, (10, 13, 18, 20)),
    ("share", 0, 0, (1, 3, 7, 10)),
    ("backward", 1, 0, (10, 14, 20, 21)),
    ("finish", 0, 0, (18, 23, 25, 26)),
    ("finish", 1, 0, (17, 21, 25, 26)),
)
TICKS = 27


def column_tiles(width):
    return [(at, min(256, width - at)) for at in range(0, width, 256)]


def kernel(
    dims,
    tok_hbm, cot_hbm, gate_hbm, up_hbm, down_hbm, gate_mask, up_mask, down_mask,
    out_hbm, grad_hbm, dgate_hbm, dup_hbm, ddown_hbm,
    wg, wu, wd, act, part, rpart, xs, xq, xt, xr, hall, outp, r1, r2f, r2s, r2r, fin, dg, du, dd,
    own_sem, o_sem, w_sem, dw_sem, ag1_s, ag1_r, ag2_s, ag2_r, cx_s, cx_r, rs1_s, rs1_r, rs2_s, rs2_r, gx1_s, gx1_r, gx2_s, gx2_r, cf_s, cf_r,
    p1_s, p1_r, p2_s, p2_r,
):
    Z, Y, X, N, R = dims
    T = Z * Y * R
    half = T // 2
    Q = half // X
    H = Q // 2
    DL, FL = wg.shape
    DH = DL // 2
    columns = (slice(0, DH), slice(DH, DL))
    row = lax.axis_index("row")
    col = lax.axis_index("col")
    z, y = row // Y, row % Y
    x, k = col // 2, col % 2

    def at_z(d):
        return (((z + d) % Z) * Y + y, col)

    def at_y(d):
        return (z * Y + (y + d) % Y, col)

    def at_x(d):
        return (row, ((x + d) % X) * 2 + k)

    other = (row, x * 2 + 1 - k)

    def remote(src, dst, ssem, rsem, where):
        return pltpu.make_async_remote_copy(
            src_ref=src, dst_ref=dst, send_sem=ssem, recv_sem=rsem, device_id=where, device_id_type=MESH
        )

    def ag1(c, g):
        return [
            remote(
                (tok_hbm, cot_hbm)[g].at[c, :, columns[h]], act.at[g, c, z, y, :, columns[h]],
                ag1_s.at[c, g], ag1_r.at[c, g], (at_y, at_z)[h](d),
            )
            for h, size in ((0, Y), (1, Z))
            for d in range(1, size)
        ]

    def ag2(c, g):
        pieces = (act.at[g, c, z, :, :, columns[0]], act.at[g, c, :, y, :, columns[1]])
        return [
            remote(pieces[h], pieces[h], ag2_s.at[c, g], ag2_r.at[c, g], (at_z, at_y)[h](d))
            for h, size in ((0, Z), (1, Y))
            for d in range(1, size)
        ]

    def cx(c, j):
        return remote(
            part.at[c, j, pl.ds((1 - k) * half, half)], rpart.at[c, j], cx_s.at[c], cx_r.at[c, j], other
        )

    def rs1(c, g):
        js = slice(0, 2) if g == 0 else slice(2, 3)
        right, left, far = (x + 1) % X, (x + X - 1) % X, (x + 2) % X
        moves = (
            (xs.at[c, far, 0, js], xq.at[c, 0, js], 1),
            (xs.at[c, far, 1, js], xq.at[c, 1, js], X - 1),
            (xs.at[c, right, 1, js], xr.at[c, 0, js], 1),
            (xs.at[c, left, 0, js], xr.at[c, 1, js], X - 1),
        )
        return [
            remote(src, dst, rs1_s.at[c, g], rs1_r.at[c, g, i], at_x(d)) for i, (src, dst, d) in enumerate(moves)
        ]

    def rs2(c, g):
        js = slice(0, 2) if g == 0 else slice(2, 3)
        return [
            remote(xt.at[c, i, js], xr.at[c, 2 + i, js], rs2_s.at[c, g], rs2_r.at[c, g, i], at_x(d))
            for i, d in ((0, 1), (1, X - 1))
        ]

    def gx1(c, g):
        js = slice(0, 1) if g == 0 else slice(1, 3)
        mine = hall.at[c, k * X + x, :, js]
        return [remote(mine, mine, gx1_s.at[c, g], gx1_r.at[c, g, i], at_x(d)) for i, d in ((0, 1), (1, X - 1))]

    def gx2(c, g):
        js = slice(0, 1) if g == 0 else slice(1, 3)
        pieces = [hall.at[c, k * X + (x + X - d) % X, i, js] for i, d in ((0, 1), (1, X - 1))]
        return [
            remote(pieces[i], pieces[i], gx2_s.at[c, g], gx2_r.at[c, g, i], at_x(d)) for i, d in ((0, 1), (1, X - 1))
        ]

    def cf(c, g, i):
        js = slice(0, 1) if g == 0 else slice(1, 3)
        block = hall.at[c, k * X + (x + (0, X - 1, 1, 2)[i]) % X, :, js]
        return remote(block, block, cf_s.at[c, g], cf_r.at[c, g, i], other)

    def p1(c, g, h):
        size, at = ((Z, at_z), (Y, at_y))[h]
        copies = []
        for d in range(1, size):
            piece = (outp.at[c, g, (z + d) % Z, :, :, columns[0]], outp.at[c, g, :, (y + d) % Y, :, columns[1]])[h]
            copies.append(remote(piece, r1.at[c, g, h, d - 1], p1_s.at[c, g, h], p1_r.at[c, g, h], at(d)))
        return copies

    def p2(c, g, h):
        size, at, me = ((Y, at_y, y), (Z, at_z, z))[h]
        return [
            remote(
                r2s.at[c, g, h, (me + d) % size], r2r.at[c, g, h, d - 1],
                p2_s.at[c, g, h], p2_r.at[c, g, h], at(d),
            )
            for d in range(1, size)
        ]

    def wait(view, sem):
        pltpu.make_async_copy(view, view, sem).wait()

    def ag1_bytes(c, g):
        return act.at[g, c, 0, 0:3]

    def ag2_bytes(c, g):
        return act.at[g, c, 0:3]

    def start(copies):
        for copy in copies:
            copy.start()

    def recv(copies):
        for copy in copies:
            copy.wait_recv()

    loads = [
        pltpu.make_async_copy(src, dst, w_sem.at[i])
        for i, (src, dst) in enumerate(((gate_hbm, wg), (up_hbm, wu), (down_hbm, wd)))
    ]
    own = [
        pltpu.make_async_copy(src, act.at[i, :, z, y], own_sem.at[i]) for i, src in enumerate((tok_hbm, cot_hbm))
    ]
    start(own)
    start(loads)
    peers = [other] + [at_x(d) for d in (1, X - 1)] + [at_y(d) for d in range(1, Y)] + [at_z(d) for d in range(1, Z)]
    barrier = pltpu.get_barrier_semaphore()
    for peer in peers:
        pl.semaphore_signal(barrier, inc=1, device_id=peer, device_id_type=MESH)
    pl.semaphore_wait(barrier, len(peers))

    def gather(c, g):
        start(ag1(c, g))

    def gather_on(c, g):
        wait(ag1_bytes(c, g), ag1_r.at[c, g])
        start(ag2(c, g))

    gather(0, 0)
    gather(0, 1)
    for copy in own:
        copy.wait()
    gather_on(0, 0)

    for copy, weight, mask in zip(loads, (wg, wu, wd), (gate_mask, up_mask, down_mask)):
        copy.wait()
        high, wide = weight.shape[0] // BLOCK, weight.shape[1] // BLOCK

        def keep_row(i, _, weight=weight, mask=mask, wide=wide):
            rows = pl.ds(pl.multiple_of(i * BLOCK, BLOCK), BLOCK)
            for j in range(wide):
                cols = slice(j * BLOCK, (j + 1) * BLOCK)
                kept = jnp.full((BLOCK, BLOCK), mask[i, j], jnp.int32).astype(F32).astype(BF16)
                weight[rows, cols] = weight[rows, cols] * kept
            return 0

        lax.fori_loop(0, high, keep_row, 0)

    def forward(c, g):
        wait(ag2_bytes(c, g), ag2_r.at[c, g])
        features = act[g, c].reshape(T, DL)
        for j in (0, 1) if g == 0 else (2,):
            for at, width in column_tiles(FL):
                if j < 2:
                    weight, sums = (wg, wu)[j][:, at : at + width], (((1,), (0,)), ((), ()))
                else:
                    weight, sums = wd[at : at + width, :], (((1,), (1,)), ((), ()))
                part[c, j, :, at : at + width] = lax.dot_general(features, weight, sums, preferred_element_type=F32)
            cx(c, j).start()

    def mine(c, j, b, h):
        at = pl.multiple_of(b * Q + h * H, H)
        here = pl.ds(pl.multiple_of(k * half + at, H), H)
        return part[c, j, here, :] + rpart[c, j, pl.ds(at, H), :]

    def share(c, g):
        for j in (0, 1) if g == 0 else (2,):
            cx(c, j).wait_recv()
            for b in range(X):
                for h in range(2):
                    xs[c, b, h, j] = mine(c, j, b, h).astype(BF16)
        start(rs1(c, g))

    def relay(c, g):
        arriving, onward = rs1(c, g), rs2(c, g)
        for i, d in ((0, 1), (1, X - 1)):
            arriving[i].wait_recv()
            for j in (0, 1) if g == 0 else (2,):
                xt[c, i, j] = (mine(c, j, (x + d) % X, i) + xq[c, i, j].astype(F32)).astype(BF16)
            onward[i].start()

    def activate(c):
        for g in range(2):
            recv(rs1(c, g)[2:])
            recv(rs2(c, g))
        block = k * X + x
        for h in range(2):

            def total(j, h=h):
                return mine(c, j, x, h) + xr[c, 1 - h, j].astype(F32) + xr[c, 2 + h, j].astype(F32)

            gate, up, back = total(0), total(1), total(2)
            s = 1.0 / (1.0 + jnp.exp(-gate))
            hall[c, block, h, 0] = (gate * s * up).astype(BF16)
            hall[c, block, h, 1] = (back * up * s * (1.0 + gate * (1.0 - s))).astype(BF16)
            hall[c, block, h, 2] = (back * gate * s).astype(BF16)
        for g in range(2):
            start(gx1(c, g))
            cf(c, g, 0).start()

    def spread(c, g):
        for i, (arriving, onward) in enumerate(zip(gx1(c, g), gx2(c, g))):
            arriving.wait_recv()
            onward.start()
            cf(c, g, 1 + i).start()

    def pass_on(c, g):
        recv(gx2(c, g))
        cf(c, g, 3).start()

    def backward(c, g):
        for i in range(4):
            cf(c, g, i).wait_recv()
        terms = ((0, wd),) if g == 0 else ((1, wg), (2, wu))
        for h in range(2):
            for at, width in column_tiles(DH):
                cols = slice(h * DH + at, h * DH + at + width)
                value = 0.0
                for j, weight in terms:
                    left = hall[c, :, :, j].reshape(T, FL)
                    if g == 0:
                        value += jnp.dot(left, weight[:, cols], preferred_element_type=F32)
                    else:
                        value += lax.dot_general(
                            left, weight[cols, :], (((1,), (1,)), ((), ())), preferred_element_type=F32
                        )
                outp[c, g, :, :, :, cols] = value.astype(BF16).reshape(Z, Y, R, width)
            start(p1(c, g, h))

    def narrow(c, g):
        for h, size, count in ((0, Z, Y), (1, Y, Z)):
            wait(r1.at[c, g, h], p1_r.at[c, g, h])
            for b in range(count):
                value = (outp[c, g, z, b, :, columns[0]], outp[c, g, b, y, :, columns[1]])[h].astype(F32)
                for d in range(1, size):
                    value = value + r1[c, g, h, d - 1, b].astype(F32)
                r2f[c, g, h, b] = value
                r2s[c, g, h, b] = value.astype(BF16)
            start(p2(c, g, h))

    def final(c, g):
        return pltpu.make_async_copy(fin.at[g, c], (out_hbm, grad_hbm)[g].at[c], o_sem.at[g, c])

    def finish(c, g):
        for h, size, me in ((0, Y, y), (1, Z, z)):
            wait(r2r.at[c, g, h], p2_r.at[c, g, h])
            value = r2f[c, g, h, me]
            for d in range(1, size):
                value = value + r2r[c, g, h, d - 1].astype(F32)
            fin[g, c, :, columns[h]] = value.astype(BF16)
        final(c, g).start()

    def weight_write(staged, hbm, n, part_of):
        rows = slice(0, 512) if part_of == 0 else slice(512, staged.shape[0])
        return pltpu.make_async_copy(staged.at[rows], hbm.at[rows], dw_sem.at[n, part_of])

    def weight_grad(staged, lhs, rhs, mask, hbm, n, part_of):
        high, wide = staged.shape
        for top, tall in column_tiles(high)[2 * part_of : 2 * part_of + 2]:
            left = lhs(top, tall)
            for at, width in column_tiles(wide):
                value = lax.dot_general(left, rhs(at, width), (((0,), (0,)), ((), ())), preferred_element_type=F32)
                for a in range(0, tall, BLOCK):
                    for b in range(0, width, BLOCK):
                        kept = jnp.full((BLOCK, BLOCK), mask[(top + a) // BLOCK, (at + b) // BLOCK], jnp.int32).astype(F32)
                        staged[top + a : top + a + BLOCK, at + b : at + b + BLOCK] = (
                            value[a : a + BLOCK, b : b + BLOCK] * kept
                        ).astype(BF16)
        weight_write(staged, hbm, n, part_of).start()

    everything = N * T

    def grads_of(j):
        return lambda at, width: hall[:, :, :, j, :, at : at + width].reshape(everything, width)

    def tokens_of(at, width):
        return act[0, :, :, :, :, at : at + width].reshape(everything, width)

    def upstream_of(at, width):
        return act[1, :, :, :, :, at : at + width].reshape(everything, width)

    def gate_grads(_, part_of):
        weight_grad(dg, tokens_of, grads_of(1), gate_mask, dgate_hbm, 0, part_of)

    def up_grads(_, part_of):
        weight_grad(du, tokens_of, grads_of(2), up_mask, dup_hbm, 1, part_of)

    def down_grads(_, part_of):
        weight_grad(dd, grads_of(0), upstream_of, down_mask, ddown_hbm, 2, part_of)

    def settle(c):
        for g in range(2):
            js = slice(0, 2) if g == 0 else slice(2, 3)
            wait(ag1_bytes(c, g), ag1_s.at[c, g])
            wait(ag2_bytes(c, g), ag2_s.at[c, g])
            wait(xs.at[c, 0:2, :, js], rs1_s.at[c, g])
            wait(xt.at[c, :, js], rs2_s.at[c, g])
        wait(rpart.at[c], cx_s.at[c])

    def settle_on(c):
        for g in range(2):
            js = slice(0, 1) if g == 0 else slice(1, 3)
            wait(hall.at[c, 0:2, :, js], gx1_s.at[c, g])
            wait(hall.at[c, 0, :, js], gx2_s.at[c, g])
            wait(hall.at[c, 0:4, :, js], cf_s.at[c, g])
            for h in range(2):
                wait(r1.at[c, g, h], p1_s.at[c, g, h])

    stages = {
        "gather": gather, "gather_on": gather_on, "forward": forward, "share": share, "relay": relay,
        "activate": activate, "spread": spread, "pass_on": pass_on, "backward": backward, "narrow": narrow,
        "finish": finish, "gate_grads": gate_grads, "up_grads": up_grads, "down_grads": down_grads,
        "settle": settle, "settle_on": settle_on,
    }

    def tick(t, _):
        for name, group, first, ticks in ORDER:
            now = False
            for at in ticks:
                now = now | (t == at)

            @pl.when(now)
            def _(stage=stages[name], group=group, first=first, ticks=ticks):
                c = first
                for at in ticks[1:]:
                    c = c + (t >= at).astype(jnp.int32)
                if group is None:
                    stage(c)
                else:
                    stage(c, group)

        return 0

    lax.fori_loop(0, TICKS, tick, 0)

    def drain(c, _):
        for g in range(2):
            for h in range(2):
                wait(r2r.at[c, g, h], p2_s.at[c, g, h])
            final(c, g).wait()
        return 0

    lax.fori_loop(0, N, drain, 0)
    for n, (staged, hbm) in enumerate(((dg, dgate_hbm), (du, dup_hbm), (dd, ddown_hbm))):
        for part_of in range(2):
            weight_write(staged, hbm, n, part_of).wait()


PIECES = 4


def publish(*refs):
    ins, outs, held, in_sem, out_sem = refs[:5], refs[5:10], refs[10:15], refs[15], refs[16]
    arriving, leaving = [], []
    for i in (2, 3, 4, 0, 1):
        pieces = PIECES if i > 1 else 1
        rows = ins[i].shape[0] // pieces
        for n in range(pieces):
            at = pl.ds(n * rows, rows)
            arriving.append(pltpu.make_async_copy(ins[i].at[at], held[i].at[at], in_sem.at[i, n]))
            leaving.append(pltpu.make_async_copy(held[i].at[at], outs[i].at[at], out_sem.at[i, n]))
    for copy in arriving:
        copy.start()
    for come, go in zip(arriving, leaving):
        come.wait()
        go.start()
    for copy in leaving:
        copy.wait()


def local(dims, tokens, cotangent, gate_weight, up_weight, down_weight, gate_mask, up_mask, down_mask):
    Z, Y, X, N, R = dims
    T = Z * Y * R
    DL, FL = gate_weight.shape
    half, Q = T // 2, T // 2 // X
    H = Q // 2
    smem, hbm = (pl.BlockSpec(memory_space=s) for s in (pltpu.SMEM, pl.ANY))
    far = pl.BlockSpec(memory_space=pltpu.HBM)
    dma = pltpu.SemaphoreType.DMA
    zy = max(Z, Y)
    ax = max(zy - 1, 1)
    results = pl.pallas_call(
        functools.partial(kernel, dims),
        out_shape=(
            jax.ShapeDtypeStruct((N, R, DL), BF16),
            jax.ShapeDtypeStruct((N, R, DL), BF16),
            jax.ShapeDtypeStruct((DL, FL), BF16),
            jax.ShapeDtypeStruct((DL, FL), BF16),
            jax.ShapeDtypeStruct((FL, DL), BF16),
        ),
        in_specs=[hbm, hbm, hbm, hbm, hbm, smem, smem, smem],
        out_specs=(hbm,) * 5,
        scratch_shapes=[
            pltpu.VMEM((DL, FL), BF16),
            pltpu.VMEM((DL, FL), BF16),
            pltpu.VMEM((FL, DL), BF16),
            pltpu.VMEM((2, N, Z, Y, R, DL), BF16),
            pltpu.VMEM((N, 3, T, FL), F32),
            pltpu.VMEM((N, 3, half, FL), F32),
            pltpu.VMEM((N, X, 2, 3, H, FL), BF16),
            pltpu.VMEM((N, 2, 3, H, FL), BF16),
            pltpu.VMEM((N, 2, 3, H, FL), BF16),
            pltpu.VMEM((N, 4, 3, H, FL), BF16),
            pltpu.VMEM((N, 2 * X, 2, 3, H, FL), BF16),
            pltpu.VMEM((N, 2, Z, Y, R, DL), BF16),
            pltpu.VMEM((N, 2, 2, ax, zy, R, DL // 2), BF16),
            pltpu.VMEM((N, 2, 2, zy, R, DL // 2), F32),
            pltpu.VMEM((N, 2, 2, zy, R, DL // 2), BF16),
            pltpu.VMEM((N, 2, 2, ax, R, DL // 2), BF16),
            pltpu.VMEM((2, N, R, DL), BF16),
            pltpu.VMEM((DL, FL), BF16),
            pltpu.VMEM((DL, FL), BF16),
            pltpu.VMEM((FL, DL), BF16),
            dma((2,)),
            dma((2, N)),
            dma((3,)),
            dma((3, 2)),
            *[dma((N, 2))] * 4,
            dma((N,)),
            dma((N, 3)),
            dma((N, 2)),
            dma((N, 2, 4)),
            *[dma((N, 2)), dma((N, 2, 2))] * 3,
            dma((N, 2)),
            dma((N, 2, 4)),
            *[dma((N, 2, 2))] * 4,
        ],
        compiler_params=pltpu.CompilerParams(
            collective_id=0, has_side_effects=True, vmem_limit_bytes=60 * 2**20
        ),
    )(tokens.reshape(N, R, DL), cotangent.reshape(N, R, DL), gate_weight, up_weight, down_weight, gate_mask, up_mask, down_mask)
    shared = pl.pallas_call(
        publish,
        out_shape=tuple(jax.ShapeDtypeStruct(r.shape, r.dtype) for r in results),
        in_specs=[far] * 5,
        out_specs=(far,) * 5,
        scratch_shapes=[*[pltpu.VMEM(r.shape, r.dtype) for r in results], dma((5, PIECES)), dma((5, PIECES))],
        compiler_params=pltpu.CompilerParams(vmem_limit_bytes=60 * 2**20),
    )(*results)
    return (shared[0].reshape(tokens.shape), shared[1].reshape(tokens.shape), *shared[2:])


def solution(mesh, dims=(4, 4, 4, 4, 16)):
    return jax.shard_map(
        functools.partial(local, dims),
        mesh=mesh,
        in_specs=(
            P("row", "col"),
            P("row", "col"),
            P("col", "row"),
            P("col", "row"),
            P("row", "col"),
            P("col", "row"),
            P("col", "row"),
            P("row", "col"),
        ),
        out_specs=(
            P("row", "col"),
            P("row", "col"),
            P("col", "row"),
            P("col", "row"),
            P("row", "col"),
        ),
        check_vma=False,
    )
```

```python
import functools

import jax
import jax.numpy as jnp
from jax import lax
from jax.experimental import pallas as pl
from jax.experimental.pallas import tpu as pltpu
from jax.sharding import PartitionSpec as P

BLOCK = 128
MESH = pl.DeviceIdType.MESH
F32 = jnp.float32
BF16 = jnp.bfloat16

ORDER = (
    ("activate", None, 0, (7, 10, 13, 17)),
    ("gather", 1, 1, (0, 1, 4)),
    ("forward", 0, 0, (1, 5, 9, 11)),
    ("gather_on", 0, 1, (1, 6, 9)),
    ("up_grads", 1, 0, (25,)),
    ("gather", 0, 1, (0, 3, 4)),
    ("down_grads", 0, 0, (26,)),
    ("spread", 0, 0, (9, 12, 16, 22)),
    ("gather_on", 1, 0, (0, 1, 3, 7)),
    ("gate_grads", 0, 0, (30,)),
    ("backward", 0, 0, (12, 15, 22, 24)),
    ("spread", 1, 0, (9, 14, 16, 22)),
    ("relay", 0, 0, (5, 8, 11, 13)),
    ("share", 1, 0, (4, 6, 7, 11)),
    ("pass_on", 1, 0, (11, 17, 20, 24)),
    ("forward", 1, 0, (2, 5, 6, 9)),
    ("settle", None, 0, (10, 20, 21, 22)),
    ("down_grads", 1, 0, (24,)),
    ("gate_grads", 1, 0, (25,)),
    ("relay", 1, 0, (5, 7, 10, 13)),
    ("share", 0, 0, (1, 5, 9, 12)),
    ("backward", 1, 0, (12, 19, 22, 24)),
    ("pass_on", 0, 0, (10, 13, 17, 22)),
    ("narrow", 0, 0, (17, 18, 24, 25)),
    ("narrow", 1, 0, (15, 24, 25, 26)),
    ("finish", 0, 0, (22, 23, 28, 29)),
    ("settle_on", None, 0, (19, 23, 26, 27)),
    ("up_grads", 0, 0, (27,)),
    ("finish", 1, 0, (23, 27, 29, 30)),
)
TICKS = 31


def column_tiles(width):
    return [(at, min(256, width - at)) for at in range(0, width, 256)]


def kernel(
    dims,
    tok_hbm, cot_hbm, gate_hbm, up_hbm, down_hbm, gate_mask, up_mask, down_mask,
    out_hbm, grad_hbm, dgate_hbm, dup_hbm, ddown_hbm,
    wg, wu, wd, act, part, rpart, xs, xq, xt, xr, hall, outp, r1, r2f, r2s, r2r, fin, dg, du, dd,
    own_sem, o_sem, w_sem, dw_sem, ag1_s, ag1_r, ag2_s, ag2_r, cx_s, cx_r, rs1_s, rs1_r, rs2_s, rs2_r, gx1_s, gx1_r, gx2_s, gx2_r, cf_s, cf_r,
    p1_s, p1_r, p2_s, p2_r,
):
    Z, Y, X, N, R = dims
    T = Z * Y * R
    half = T // 2
    Q = half // X
    H = Q // 2
    DL, FL = wg.shape
    DH = DL // 2
    columns = (slice(0, DH), slice(DH, DL))
    row = lax.axis_index("row")
    col = lax.axis_index("col")
    z, y = row // Y, row % Y
    x, k = col // 2, col % 2

    def at_z(d):
        return (((z + d) % Z) * Y + y, col)

    def at_y(d):
        return (z * Y + (y + d) % Y, col)

    def at_x(d):
        return (row, ((x + d) % X) * 2 + k)

    other = (row, x * 2 + 1 - k)

    def remote(src, dst, ssem, rsem, where):
        return pltpu.make_async_remote_copy(
            src_ref=src, dst_ref=dst, send_sem=ssem, recv_sem=rsem, device_id=where, device_id_type=MESH
        )

    def ag1(c, g):
        return [
            remote(
                (tok_hbm, cot_hbm)[g].at[c, :, columns[h]], act.at[g, c, z, y, :, columns[h]],
                ag1_s.at[c, g], ag1_r.at[c, g], (at_y, at_z)[h](d),
            )
            for h, size in ((0, Y), (1, Z))
            for d in range(1, size)
        ]

    def ag2(c, g):
        pieces = (act.at[g, c, z, :, :, columns[0]], act.at[g, c, :, y, :, columns[1]])
        return [
            remote(pieces[h], pieces[h], ag2_s.at[c, g], ag2_r.at[c, g], (at_z, at_y)[h](d))
            for h, size in ((0, Z), (1, Y))
            for d in range(1, size)
        ]

    def cx(c, j):
        return remote(
            part.at[c, j, pl.ds((1 - k) * half, half)], rpart.at[c, j], cx_s.at[c], cx_r.at[c, j], other
        )

    def rs1(c, g):
        js = slice(0, 2) if g == 0 else slice(2, 3)
        right, left, far = (x + 1) % X, (x + X - 1) % X, (x + 2) % X
        moves = (
            (xs.at[c, far, 0, js], xq.at[c, 0, js], 1),
            (xs.at[c, far, 1, js], xq.at[c, 1, js], X - 1),
            (xs.at[c, right, 1, js], xr.at[c, 0, js], 1),
            (xs.at[c, left, 0, js], xr.at[c, 1, js], X - 1),
        )
        return [
            remote(src, dst, rs1_s.at[c, g], rs1_r.at[c, g, i], at_x(d)) for i, (src, dst, d) in enumerate(moves)
        ]

    def rs2(c, g):
        js = slice(0, 2) if g == 0 else slice(2, 3)
        return [
            remote(xt.at[c, i, js], xr.at[c, 2 + i, js], rs2_s.at[c, g], rs2_r.at[c, g, i], at_x(d))
            for i, d in ((0, 1), (1, X - 1))
        ]

    def gx1(c, g):
        js = slice(0, 1) if g == 0 else slice(1, 3)
        mine = hall.at[c, k * X + x, :, js]
        return [remote(mine, mine, gx1_s.at[c, g], gx1_r.at[c, g, i], at_x(d)) for i, d in ((0, 1), (1, X - 1))]

    def gx2(c, g):
        js = slice(0, 1) if g == 0 else slice(1, 3)
        pieces = [hall.at[c, k * X + (x + X - d) % X, i, js] for i, d in ((0, 1), (1, X - 1))]
        return [
            remote(pieces[i], pieces[i], gx2_s.at[c, g], gx2_r.at[c, g, i], at_x(d)) for i, d in ((0, 1), (1, X - 1))
        ]

    def cf(c, g, i):
        js = slice(0, 1) if g == 0 else slice(1, 3)
        block = hall.at[c, k * X + (x + (0, X - 1, 1, 2)[i]) % X, :, js]
        return remote(block, block, cf_s.at[c, g], cf_r.at[c, g, i], other)

    def p1(c, g, h):
        size, at = ((Z, at_z), (Y, at_y))[h]
        copies = []
        for d in range(1, size):
            piece = (outp.at[c, g, (z + d) % Z, :, :, columns[0]], outp.at[c, g, :, (y + d) % Y, :, columns[1]])[h]
            copies.append(remote(piece, r1.at[c, g, h, d - 1], p1_s.at[c, g, h], p1_r.at[c, g, h], at(d)))
        return copies

    def p2(c, g, h):
        size, at, me = ((Y, at_y, y), (Z, at_z, z))[h]
        return [
            remote(
                r2s.at[c, g, h, (me + d) % size], r2r.at[c, g, h, d - 1],
                p2_s.at[c, g, h], p2_r.at[c, g, h], at(d),
            )
            for d in range(1, size)
        ]

    def wait(view, sem):
        pltpu.make_async_copy(view, view, sem).wait()

    def ag1_bytes(c, g):
        return act.at[g, c, 0, 0:3]

    def ag2_bytes(c, g):
        return act.at[g, c, 0:3]

    def start(copies):
        for copy in copies:
            copy.start()

    def recv(copies):
        for copy in copies:
            copy.wait_recv()

    loads = [
        pltpu.make_async_copy(src, dst, w_sem.at[i])
        for i, (src, dst) in enumerate(((gate_hbm, wg), (up_hbm, wu), (down_hbm, wd)))
    ]
    own = [
        pltpu.make_async_copy(src, act.at[i, :, z, y], own_sem.at[i]) for i, src in enumerate((tok_hbm, cot_hbm))
    ]
    start(own)
    start(loads)
    peers = [other] + [at_x(d) for d in (1, X - 1)] + [at_y(d) for d in range(1, Y)] + [at_z(d) for d in range(1, Z)]
    barrier = pltpu.get_barrier_semaphore()
    for peer in peers:
        pl.semaphore_signal(barrier, inc=1, device_id=peer, device_id_type=MESH)
    pl.semaphore_wait(barrier, len(peers))

    def gather(c, g):
        start(ag1(c, g))

    def gather_on(c, g):
        wait(ag1_bytes(c, g), ag1_r.at[c, g])
        start(ag2(c, g))

    gather(0, 0)
    gather(0, 1)
    for copy in own:
        copy.wait()
    gather_on(0, 0)

    for copy, weight, mask in zip(loads, (wg, wu, wd), (gate_mask, up_mask, down_mask)):
        copy.wait()
        high, wide = weight.shape[0] // BLOCK, weight.shape[1] // BLOCK

        def keep_row(i, _, weight=weight, mask=mask, wide=wide):
            rows = pl.ds(pl.multiple_of(i * BLOCK, BLOCK), BLOCK)
            for j in range(wide):
                cols = slice(j * BLOCK, (j + 1) * BLOCK)
                kept = jnp.full((BLOCK, BLOCK), mask[i, j], jnp.int32).astype(F32).astype(BF16)
                weight[rows, cols] = weight[rows, cols] * kept
            return 0

        lax.fori_loop(0, high, keep_row, 0)

    def forward(c, g):
        wait(ag2_bytes(c, g), ag2_r.at[c, g])
        features = act[g, c].reshape(T, DL)
        for j in (0, 1) if g == 0 else (2,):
            for at, width in column_tiles(FL):
                if j < 2:
                    weight, sums = (wg, wu)[j][:, at : at + width], (((1,), (0,)), ((), ()))
                else:
                    weight, sums = wd[at : at + width, :], (((1,), (1,)), ((), ()))
                part[c, j, :, at : at + width] = lax.dot_general(features, weight, sums, preferred_element_type=F32)
            cx(c, j).start()

    def mine(c, j, b, h):
        at = pl.multiple_of(b * Q + h * H, H)
        here = pl.ds(pl.multiple_of(k * half + at, H), H)
        return part[c, j, here, :] + rpart[c, j, pl.ds(at, H), :]

    def share(c, g):
        for j in (0, 1) if g == 0 else (2,):
            cx(c, j).wait_recv()
            for b in range(X):
                for h in range(2):
                    xs[c, b, h, j] = mine(c, j, b, h).astype(BF16)
        start(rs1(c, g))

    def relay(c, g):
        arriving, onward = rs1(c, g), rs2(c, g)
        for i, d in ((0, 1), (1, X - 1)):
            arriving[i].wait_recv()
            for j in (0, 1) if g == 0 else (2,):
                xt[c, i, j] = (mine(c, j, (x + d) % X, i) + xq[c, i, j].astype(F32)).astype(BF16)
            onward[i].start()

    def activate(c):
        for g in range(2):
            recv(rs1(c, g)[2:])
            recv(rs2(c, g))
        block = k * X + x
        for h in range(2):

            def total(j, h=h):
                return mine(c, j, x, h) + xr[c, 1 - h, j].astype(F32) + xr[c, 2 + h, j].astype(F32)

            gate, up, back = total(0), total(1), total(2)
            s = 1.0 / (1.0 + jnp.exp(-gate))
            hall[c, block, h, 0] = (gate * s * up).astype(BF16)
            hall[c, block, h, 1] = (back * up * s * (1.0 + gate * (1.0 - s))).astype(BF16)
            hall[c, block, h, 2] = (back * gate * s).astype(BF16)
        for g in range(2):
            start(gx1(c, g))
            cf(c, g, 0).start()

    def spread(c, g):
        for i, (arriving, onward) in enumerate(zip(gx1(c, g), gx2(c, g))):
            arriving.wait_recv()
            onward.start()
            cf(c, g, 1 + i).start()

    def pass_on(c, g):
        recv(gx2(c, g))
        cf(c, g, 3).start()

    def backward(c, g):
        for i in range(4):
            cf(c, g, i).wait_recv()
        terms = ((0, wd),) if g == 0 else ((1, wg), (2, wu))
        for h in range(2):
            for at, width in column_tiles(DH):
                cols = slice(h * DH + at, h * DH + at + width)
                value = 0.0
                for j, weight in terms:
                    left = hall[c, :, :, j].reshape(T, FL)
                    if g == 0:
                        value += jnp.dot(left, weight[:, cols], preferred_element_type=F32)
                    else:
                        value += lax.dot_general(
                            left, weight[cols, :], (((1,), (1,)), ((), ())), preferred_element_type=F32
                        )
                outp[c, g, :, :, :, cols] = value.astype(BF16).reshape(Z, Y, R, width)
            start(p1(c, g, h))

    def narrow(c, g):
        for h, size, count in ((0, Z, Y), (1, Y, Z)):
            wait(r1.at[c, g, h], p1_r.at[c, g, h])
            for b in range(count):
                value = (outp[c, g, z, b, :, columns[0]], outp[c, g, b, y, :, columns[1]])[h].astype(F32)
                for d in range(1, size):
                    value = value + r1[c, g, h, d - 1, b].astype(F32)
                r2f[c, g, h, b] = value
                r2s[c, g, h, b] = value.astype(BF16)
            start(p2(c, g, h))

    def final(c, g):
        return pltpu.make_async_copy(fin.at[g, c], (out_hbm, grad_hbm)[g].at[c], o_sem.at[g, c])

    def finish(c, g):
        for h, size, me in ((0, Y, y), (1, Z, z)):
            wait(r2r.at[c, g, h], p2_r.at[c, g, h])
            value = r2f[c, g, h, me]
            for d in range(1, size):
                value = value + r2r[c, g, h, d - 1].astype(F32)
            fin[g, c, :, columns[h]] = value.astype(BF16)
        final(c, g).start()

    def weight_write(staged, hbm, n, part_of):
        rows = slice(0, 512) if part_of == 0 else slice(512, staged.shape[0])
        return pltpu.make_async_copy(staged.at[rows], hbm.at[rows], dw_sem.at[n, part_of])

    def weight_grad(staged, lhs, rhs, mask, hbm, n, part_of):
        high, wide = staged.shape
        for top, tall in column_tiles(high)[2 * part_of : 2 * part_of + 2]:
            left = lhs(top, tall)
            for at, width in column_tiles(wide):
                value = lax.dot_general(left, rhs(at, width), (((0,), (0,)), ((), ())), preferred_element_type=F32)
                for a in range(0, tall, BLOCK):
                    for b in range(0, width, BLOCK):
                        kept = jnp.full((BLOCK, BLOCK), mask[(top + a) // BLOCK, (at + b) // BLOCK], jnp.int32).astype(F32)
                        staged[top + a : top + a + BLOCK, at + b : at + b + BLOCK] = (
                            value[a : a + BLOCK, b : b + BLOCK] * kept
                        ).astype(BF16)
        weight_write(staged, hbm, n, part_of).start()

    everything = N * T

    def grads_of(j):
        return lambda at, width: hall[:, :, :, j, :, at : at + width].reshape(everything, width)

    def tokens_of(at, width):
        return act[0, :, :, :, :, at : at + width].reshape(everything, width)

    def upstream_of(at, width):
        return act[1, :, :, :, :, at : at + width].reshape(everything, width)

    def gate_grads(_, part_of):
        weight_grad(dg, tokens_of, grads_of(1), gate_mask, dgate_hbm, 0, part_of)

    def up_grads(_, part_of):
        weight_grad(du, tokens_of, grads_of(2), up_mask, dup_hbm, 1, part_of)

    def down_grads(_, part_of):
        weight_grad(dd, grads_of(0), upstream_of, down_mask, ddown_hbm, 2, part_of)

    def settle(c):
        for g in range(2):
            js = slice(0, 2) if g == 0 else slice(2, 3)
            wait(ag1_bytes(c, g), ag1_s.at[c, g])
            wait(ag2_bytes(c, g), ag2_s.at[c, g])
            wait(xs.at[c, 0:2, :, js], rs1_s.at[c, g])
            wait(xt.at[c, :, js], rs2_s.at[c, g])
        wait(rpart.at[c], cx_s.at[c])

    def settle_on(c):
        for g in range(2):
            js = slice(0, 1) if g == 0 else slice(1, 3)
            wait(hall.at[c, 0:2, :, js], gx1_s.at[c, g])
            wait(hall.at[c, 0, :, js], gx2_s.at[c, g])
            wait(hall.at[c, 0:4, :, js], cf_s.at[c, g])
            for h in range(2):
                wait(r1.at[c, g, h], p1_s.at[c, g, h])

    stages = {
        "gather": gather, "gather_on": gather_on, "forward": forward, "share": share, "relay": relay,
        "activate": activate, "spread": spread, "pass_on": pass_on, "backward": backward, "narrow": narrow,
        "finish": finish, "gate_grads": gate_grads, "up_grads": up_grads, "down_grads": down_grads,
        "settle": settle, "settle_on": settle_on,
    }

    def tick(t, _):
        for name, group, first, ticks in ORDER:
            now = False
            for at in ticks:
                now = now | (t == at)

            @pl.when(now)
            def _(stage=stages[name], group=group, first=first, ticks=ticks):
                c = first
                for at in ticks[1:]:
                    c = c + (t >= at).astype(jnp.int32)
                if group is None:
                    stage(c)
                else:
                    stage(c, group)

        return 0

    lax.fori_loop(0, TICKS, tick, 0)

    def drain(c, _):
        for g in range(2):
            for h in range(2):
                wait(r2r.at[c, g, h], p2_s.at[c, g, h])
            final(c, g).wait()
        return 0

    lax.fori_loop(0, N, drain, 0)
    for n, (staged, hbm) in enumerate(((dg, dgate_hbm), (du, dup_hbm), (dd, ddown_hbm))):
        for part_of in range(2):
            weight_write(staged, hbm, n, part_of).wait()


PIECES = 4


def publish(*refs):
    ins, outs, held, in_sem, out_sem = refs[:5], refs[5:10], refs[10:15], refs[15], refs[16]
    arriving, leaving = [], []
    for i in (2, 3, 4, 0, 1):
        pieces = PIECES if i > 1 else 1
        rows = ins[i].shape[0] // pieces
        for n in range(pieces):
            at = pl.ds(n * rows, rows)
            arriving.append(pltpu.make_async_copy(ins[i].at[at], held[i].at[at], in_sem.at[i, n]))
            leaving.append(pltpu.make_async_copy(held[i].at[at], outs[i].at[at], out_sem.at[i, n]))
    for copy in arriving:
        copy.start()
    for come, go in zip(arriving, leaving):
        come.wait()
        go.start()
    for copy in leaving:
        copy.wait()


def local(dims, tokens, cotangent, gate_weight, up_weight, down_weight, gate_mask, up_mask, down_mask):
    Z, Y, X, N, R = dims
    T = Z * Y * R
    DL, FL = gate_weight.shape
    half, Q = T // 2, T // 2 // X
    H = Q // 2
    smem, hbm = (pl.BlockSpec(memory_space=s) for s in (pltpu.SMEM, pl.ANY))
    far = pl.BlockSpec(memory_space=pltpu.HBM)
    dma = pltpu.SemaphoreType.DMA
    zy = max(Z, Y)
    ax = max(zy - 1, 1)
    results = pl.pallas_call(
        functools.partial(kernel, dims),
        out_shape=(
            jax.ShapeDtypeStruct((N, R, DL), BF16),
            jax.ShapeDtypeStruct((N, R, DL), BF16),
            jax.ShapeDtypeStruct((DL, FL), BF16),
            jax.ShapeDtypeStruct((DL, FL), BF16),
            jax.ShapeDtypeStruct((FL, DL), BF16),
        ),
        in_specs=[hbm, hbm, hbm, hbm, hbm, smem, smem, smem],
        out_specs=(hbm,) * 5,
        scratch_shapes=[
            pltpu.VMEM((DL, FL), BF16),
            pltpu.VMEM((DL, FL), BF16),
            pltpu.VMEM((FL, DL), BF16),
            pltpu.VMEM((2, N, Z, Y, R, DL), BF16),
            pltpu.VMEM((N, 3, T, FL), F32),
            pltpu.VMEM((N, 3, half, FL), F32),
            pltpu.VMEM((N, X, 2, 3, H, FL), BF16),
            pltpu.VMEM((N, 2, 3, H, FL), BF16),
            pltpu.VMEM((N, 2, 3, H, FL), BF16),
            pltpu.VMEM((N, 4, 3, H, FL), BF16),
            pltpu.VMEM((N, 2 * X, 2, 3, H, FL), BF16),
            pltpu.VMEM((N, 2, Z, Y, R, DL), BF16),
            pltpu.VMEM((N, 2, 2, ax, zy, R, DL // 2), BF16),
            pltpu.VMEM((N, 2, 2, zy, R, DL // 2), F32),
            pltpu.VMEM((N, 2, 2, zy, R, DL // 2), BF16),
            pltpu.VMEM((N, 2, 2, ax, R, DL // 2), BF16),
            pltpu.VMEM((2, N, R, DL), BF16),
            pltpu.VMEM((DL, FL), BF16),
            pltpu.VMEM((DL, FL), BF16),
            pltpu.VMEM((FL, DL), BF16),
            dma((2,)),
            dma((2, N)),
            dma((3,)),
            dma((3, 2)),
            *[dma((N, 2))] * 4,
            dma((N,)),
            dma((N, 3)),
            dma((N, 2)),
            dma((N, 2, 4)),
            *[dma((N, 2)), dma((N, 2, 2))] * 3,
            dma((N, 2)),
            dma((N, 2, 4)),
            *[dma((N, 2, 2))] * 4,
        ],
        compiler_params=pltpu.CompilerParams(
            collective_id=0, has_side_effects=True, vmem_limit_bytes=60 * 2**20
        ),
    )(tokens.reshape(N, R, DL), cotangent.reshape(N, R, DL), gate_weight, up_weight, down_weight, gate_mask, up_mask, down_mask)
    shared = pl.pallas_call(
        publish,
        out_shape=tuple(jax.ShapeDtypeStruct(r.shape, r.dtype) for r in results),
        in_specs=[far] * 5,
        out_specs=(far,) * 5,
        scratch_shapes=[*[pltpu.VMEM(r.shape, r.dtype) for r in results], dma((5, PIECES)), dma((5, PIECES))],
        compiler_params=pltpu.CompilerParams(vmem_limit_bytes=60 * 2**20),
    )(*results)
    return (shared[0].reshape(tokens.shape), shared[1].reshape(tokens.shape), *shared[2:])


def solution(mesh, dims=(4, 4, 4, 4, 16)):
    return jax.shard_map(
        functools.partial(local, dims),
        mesh=mesh,
        in_specs=(
            P("row", "col"),
            P("row", "col"),
            P("col", "row"),
            P("col", "row"),
            P("row", "col"),
            P("col", "row"),
            P("col", "row"),
            P("row", "col"),
        ),
        out_specs=(
            P("row", "col"),
            P("row", "col"),
            P("col", "row"),
            P("col", "row"),
            P("row", "col"),
        ),
        check_vma=False,
    )
```
